256 devices in a mesh: dp: 16 (over x_lo, y, core), mp: 16 (over x_hi, z).
Axes of the slice: x: 4 (x_hi: 2, x_lo: 2; x = x_hi * 2 + x_lo), y: 4, z: 8, core: 2. Of those that a mesh axis runs over, the one named last changes fastest.
Arguments:
- patches: bfloat16 [8192, 6144], P('dp', 'mp'), may hold values from -1000 to 1000
- norm_gain: bfloat16 [6144], P('mp'), may hold values from 0.099609375 to 1.8984375
- qkv_weight: bfloat16 [6144, 12288], P(None, 'mp'), may hold values from -0.078125 to 0.078125
- qk_gain: float32 [2, 32, 128], P(None, 'mp'), may hold values from 0.6 to 5.5
- context_grad: bfloat16 [8192, 4096], P('dp', 'mp'), may hold values from -6 to 6
Outputs:
- context: bfloat16 [8192, 4096], P('dp', 'mp')
- input_grad: bfloat16 [8192, 6144], P('dp', 'mp')
- weight_grad: bfloat16 [6144, 12288], P('dp', 'mp')
- norm_gain_grad: float32 [6144], P('mp')
- qk_gain_grad: float32 [2, 32, 128], P(None, 'mp')
The draws below stay inside these ranges and needn't reach their ends.
All inputs are finite; a program needn't handle non-finite values.
Results may differ from the reference program's by a relative error of at most 0.025.
The reference program's roundings to bfloat16 on the way count: a program that leaves them out, or rounds other values in their place, can miss the bound.
Values may be sent and summed in bfloat16 or wider, within the bound.
A program may use at most 128 MiB of HBM per device.

```python
import math
import jax
import jax.numpy as jnp
from jax import lax

D = 6144
HEAD_DIM = 128
PATCHES = 256
HEADS_DEV = 2
HEADS = 32
IMAGES = 32
TOKENS = 8192


def draw_patches(key, part):
    key = jax.random.fold_in(key, 3)
    base_key, col_key, row_key = jax.random.split(key, 3)
    col_pos = jnp.arange(D, dtype=jnp.float32) / D
    col_scale = jnp.exp(col_pos[None, :] * math.log(10.0) + jax.random.uniform(col_key, (1, D), jnp.float32, -0.69, 0.69))
    row_scale = jnp.exp(jax.random.uniform(row_key, (TOKENS, 1), jnp.float32, 0.0, math.log(10.0)))
    base = jnp.clip(jax.random.normal(base_key, (TOKENS, D), jnp.float32), -4.5, 4.5)
    return (base * row_scale * col_scale).astype(jnp.bfloat16)


def draw_qk_gain(key, part):
    key = jax.random.fold_in(key, 7)
    return jax.random.uniform(key, (2, HEADS, HEAD_DIM), jnp.float32, 0.6, 1.6)


def levels(key, shape, shards, smallest, largest):
    def one(position, shards_of):
        draws = jax.random.uniform(jax.random.fold_in(jax.random.fold_in(key, 6), position), (shards_of,), jnp.float32, smallest / len(shards), largest / len(shards))
        return jnp.repeat(jnp.exp(draws), shape[position] // shards_of).reshape((-1,) + (1,) * (len(shape) - position - 1))

    level = one(*shards[0])
    for cut in shards[1:]:
        level = level * one(*cut)
    return level


def scatter_about(key, shape, scale, most, cuts=(), held_as=jnp.bfloat16):
    entries = jax.random.normal(key, shape, jnp.float32) * scale
    if len(cuts) > 0:
        entries = levels(key, shape, cuts, -0.22, 0.18) * entries
    return jnp.clip(entries, min=-most, max=most).astype(held_as)


def setup_inputs(seed: int = 0) -> dict:
    key_list = jax.random.split(jax.random.key(seed), 6)
    return {
        "patches": draw_patches(jax.random.fold_in(key_list[5], 71), 0),
        "norm_gain": jnp.clip(1.0 + 0.18 * jax.random.normal(key_list[1], (D,), jnp.float32), 0.099609375, 1.8984375).astype(jnp.bfloat16),
        "qkv_weight": scatter_about(key_list[2], (D, 3 * HEADS * HEAD_DIM), D ** -0.5, 0.078125, ((1, 16),)),
        "qk_gain": draw_qk_gain(jax.random.fold_in(key_list[5], 71), 0),
        "context_grad": scatter_about(key_list[4], (TOKENS, HEADS * HEAD_DIM), 1.0, 6.0, ((0, 16), (1, 16))),
    }


epsilon = 1e-06

def head_norm(values):
    centered = values - lax.optimization_barrier(jnp.mean(values, axis=-1, keepdims=True))
    inv_std = lax.rsqrt(lax.optimization_barrier(jnp.mean(centered * centered, axis=-1, keepdims=True)) + epsilon)
    return (centered * inv_std, inv_std)

def norm_back(incoming_grad, unit_vals, inv_std):
    mean_grad = lax.optimization_barrier(jnp.mean(incoming_grad, axis=-1, keepdims=True))
    second = lax.optimization_barrier(jnp.mean(incoming_grad * unit_vals, axis=-1, keepdims=True))
    return inv_std * (incoming_grad - mean_grad - unit_vals * second)

def attend(packed, head_gains, incoming_grad):
    q_unit, q_inv = head_norm(packed[:, :, 0])
    k_unit, k_inv = head_norm(packed[:, :, 1])
    query_normed = (q_unit * head_gains[0]).astype(jnp.bfloat16)
    key_normed = (k_unit * head_gains[1]).astype(jnp.bfloat16)
    value_narrow = packed[:, :, 2].astype(jnp.bfloat16)
    scale_factor = 1.0 / math.sqrt(packed.shape[-1])
    logit_scores = jnp.einsum('tih,tjh->tij', query_normed.astype(jnp.float32), key_normed.astype(jnp.float32)) * scale_factor
    shifted = logit_scores - lax.optimization_barrier(jnp.max(logit_scores, axis=-1, keepdims=True))
    exp_scores = jnp.exp(shifted)
    attn_probs = exp_scores / lax.optimization_barrier(jnp.sum(exp_scores, axis=-1, keepdims=True))
    probability_narrow = attn_probs.astype(jnp.bfloat16)
    context = jnp.einsum('rin,rnt->rit', probability_narrow.astype(jnp.float32), value_narrow.astype(jnp.float32)).astype(jnp.bfloat16)
    upstream_widened = incoming_grad.astype(jnp.float32)
    probability_grad = jnp.einsum('tih,tjh->tij', upstream_widened, value_narrow.astype(jnp.float32))
    value_grad = jnp.einsum('smi,smy->siy', probability_narrow.astype(jnp.float32), upstream_widened)
    row_delta = lax.optimization_barrier(jnp.sum(attn_probs * probability_grad, axis=-1, keepdims=True))
    score_grad = (attn_probs * (probability_grad - row_delta)).astype(jnp.bfloat16)
    normed_query_grad = jnp.einsum('rin,rnt->rit', score_grad.astype(jnp.float32), key_normed.astype(jnp.float32)) * scale_factor
    normed_key_grad = jnp.einsum('smi,smy->siy', score_grad.astype(jnp.float32), query_normed.astype(jnp.float32)) * scale_factor
    gain_grad = jnp.stack([lax.optimization_barrier(jnp.sum(normed_query_grad * q_unit, axis=(0, 1))), lax.optimization_barrier(jnp.sum(normed_key_grad * k_unit, axis=(0, 1)))])
    d_query = norm_back(normed_query_grad * head_gains[0], q_unit, q_inv)
    d_key = norm_back(normed_key_grad * head_gains[1], k_unit, k_inv)
    packed_grad = jnp.stack([d_query, d_key, value_grad], axis=2).astype(jnp.bfloat16)
    return (context, packed_grad, gain_grad)

def reference(patches, norm_gain, qkv_weight, qk_gain, context_grad):
    row_vals = patches.astype(jnp.float32)
    row_mean = lax.optimization_barrier(jnp.mean(row_vals, axis=1, keepdims=True))
    centered = row_vals - row_mean
    inv_std = lax.rsqrt(lax.optimization_barrier(jnp.mean(centered * centered, axis=1, keepdims=True)) + epsilon)
    unit_rows = centered * inv_std
    gain_wide = norm_gain.astype(jnp.float32)
    normed = (unit_rows * gain_wide).astype(jnp.bfloat16)
    projected = jnp.dot(normed, qkv_weight, preferred_element_type=jnp.float32)
    packed = projected.reshape(IMAGES, PATCHES, HEADS, 3, HEAD_DIM).transpose(2, 0, 1, 3, 4)
    incoming_grad = context_grad.reshape(IMAGES, PATCHES, HEADS, HEAD_DIM).transpose(2, 0, 1, 3)
    head_gains = qk_gain.transpose(1, 0, 2)
    context, packed_grad, gain_grad = lax.map(lambda head_inputs: attend(*head_inputs), (packed, head_gains, incoming_grad))
    context = context.transpose(1, 2, 0, 3).reshape(TOKENS, HEADS * HEAD_DIM)
    qkv_grad = packed_grad.transpose(1, 2, 0, 3, 4).reshape(TOKENS, HEADS * 3 * HEAD_DIM)
    qk_gain_grad = gain_grad.transpose(1, 0, 2)
    weight_grad = lax.dot_general(normed, qkv_grad, (((0,), (0,)), ((), ())), preferred_element_type=jnp.float32).astype(jnp.bfloat16)
    group_cols = HEADS_DEV * 3 * HEAD_DIM
    normed_grad = jnp.zeros((TOKENS, D), jnp.float32)
    for member in range(HEADS // HEADS_DEV):
        part_grad = qkv_grad[:, member * group_cols:(member + 1) * group_cols]
        part_weight = qkv_weight[:, member * group_cols:(member + 1) * group_cols]
        partial_term = lax.dot_general(part_grad, part_weight, (((1,), (1,)), ((), ())), preferred_element_type=jnp.float32).astype(jnp.bfloat16)
        partial_term = lax.optimization_barrier(partial_term)
        normed_grad = normed_grad + partial_term.astype(jnp.float32)
    norm_gain_grad = lax.optimization_barrier(jnp.sum(normed_grad * unit_rows, axis=0))
    input_grad = norm_back(normed_grad * gain_wide, unit_rows, inv_std).astype(jnp.bfloat16)
    return (context, input_grad, weight_grad, norm_gain_grad, qk_gain_grad)
```

```python
import functools
import math

import jax
import jax.numpy as jnp
from jax import lax
from jax.experimental import pallas as pl
from jax.experimental.pallas import tpu as pltpu
from jax.sharding import PartitionSpec as P

HEAD_DIM = 128
IMG = 256
NIMG = 2
TOK = IMG * NIMG
FB = 384
NB = 16
D = FB * NB
HC = 768
GR = 16
ROWS = GR + TOK
HALF = IMG // 2
XC = 384
EPS = 1e-6
SCALE = 1.0 / math.sqrt(HEAD_DIM)
MESH = pl.DeviceIdType.MESH
F32 = jnp.float32
BF16 = jnp.bfloat16
NSEM = 192


def dot_t(a, b):
    return lax.dot_general(a, b, (((1,), (1,)), ((), ())), preferred_element_type=F32)


def t_dot(a, b):
    return lax.dot_general(a, b, (((0,), (0,)), ((), ())), preferred_element_type=F32)


def kernel(
    p_hbm, gain_ref, w_hbm, qkg_ref, cg_ref,
    ctx_ref, ig_ref, wg_ref, small_ref,
    xg, wv, nrm, nrm_t, proj, qkvg, mu, inv,
    cr, ci, t1, cxs, cxr, cys, cyr, plane1,
    ds, dr, dxr, dxl, dyr,
    sxs, sxr, trans, sms, smr,
    ss, rs, ls,
):
    d = lax.axis_index("dp")
    m = lax.axis_index("mp")
    xl, y, core = d // 8, (d // 2) % 4, d % 2
    xh, z = m // 8, m % 8
    count = [0]
    sends = []

    def at(xl_=None, y_=None, core_=None, xh_=None, z_=None):
        xl_ = xl if xl_ is None else xl_
        y_ = y if y_ is None else y_
        core_ = core if core_ is None else core_
        xh_ = xh if xh_ is None else xh_
        z_ = z if z_ is None else z_
        return {"dp": xl_ * 8 + y_ * 2 + core_, "mp": xh_ * 8 + z_}

    z_dev = {1: at(z_=(z + 1) % 8), -1: at(z_=(z + 7) % 8)}
    y_dev = {1: at(y_=(y + 1) % 4), -1: at(y_=(y + 3) % 4)}
    xh_dev = at(xh_=1 - xh)
    xl_dev = at(xl_=1 - xl)
    core_dev = at(core_=1 - core)

    def send(src, dst, dev):
        i = count[0]
        count[0] += 1
        copy = pltpu.make_async_remote_copy(
            src_ref=src, dst_ref=dst, send_sem=ss.at[i], recv_sem=rs.at[i],
            device_id=dev, device_id_type=MESH,
        )
        copy.start()
        sends.append(copy)
        return copy

    own = pltpu.make_async_copy(p_hbm, xg.at[m, pl.ds(GR, TOK)], ls.at[0])
    own.start()
    weights = pltpu.make_async_copy(w_hbm, wv, ls.at[1])
    weights.start()
    xg[m, pl.ds(0, GR), :] = jnp.broadcast_to(gain_ref[...], (GR, FB))
    barrier = pltpu.get_barrier_semaphore()
    for o in range(1, NB):
        pl.semaphore_signal(barrier, inc=1, device_id={"dp": d, "mp": (m + o) % NB}, device_id_type=MESH)
        pl.semaphore_signal(barrier, inc=1, device_id={"dp": (d + o) % NB, "mp": m}, device_id_type=MESH)
    pl.semaphore_wait(barrier, 2 * (NB - 1))
    own.wait()

    def blk(plane, zz):
        return (xh if plane == 0 else 1 - xh) * 8 + (zz + 16) % 8

    def span(img, part):
        lo0 = 0 if img == 0 else GR + IMG
        mid = GR + img * IMG + HALF
        end = GR + (img + 1) * IMG
        return {
            "full": (lo0, end - lo0),
            "lo": (lo0, mid - lo0),
            "hi": (mid, end - mid),
            "hi0": (mid, HALF // 2),
            "hi1": (mid + HALF // 2, HALF // 2),
        }[part]

    ring = {}
    xrecv = {0: [], 1: []}

    def send_block(img, plane, origin_z, part, dev):
        r, n = span(img, part)
        ref = xg.at[blk(plane, origin_z), pl.ds(r, n)]
        return send(ref, ref, dev)

    def hop_parts(plane):
        if plane == 0:
            return {1: "full", -1: "full"}, {1: "lo", -1: "hi"}
        return {1: "hi", -1: "hi"}, {1: "hi0", -1: "hi1"}

    def forward(img, plane, s):
        parts = hop_parts(plane)[0 if s < 4 else 1]
        for dr_ in (1, -1):
            ring[(img, plane, s, dr_)] = send_block(img, plane, z - (s - 1) * dr_, parts[dr_], z_dev[dr_])

    def arrive(img, plane, s):
        for dr_ in (1, -1):
            ring[(img, plane, s, dr_)].wait_recv()

    def ag0(img):
        ring[(img, "x")] = send_block(img, 0, z, "hi", xh_dev)
        forward(img, 0, 1)
        xrecv[img].append(send_block(img, 0, z, "lo", xh_dev))

    def ag1(img):
        ring[(img, "x")].wait_recv()
        forward(img, 1, 1)

    def ag_hop(img, plane, s):
        arrive(img, plane, s)
        if s < 4:
            forward(img, plane, s + 1)
        if plane == 0:
            for dr_ in (1, -1) if s < 4 else (1,):
                xrecv[img].append(send_block(img, 0, z - s * dr_, "lo", xh_dev))

    def ag_end(img):
        for c in xrecv[img]:
            c.wait_recv()

    def norm(img):
        @pl.loop(0, IMG // 64)
        def _(c):
            r = pl.ds(pl.multiple_of(GR + img * IMG + c * 64, 16), 64)
            shift = jnp.mean(xg[0, r, :].astype(F32), axis=1, keepdims=True)

            def stat(k, carry):
                v = xg[k, r, :].astype(F32) - shift
                w = v * v
                fold = lambda t: t[:, :128] + t[:, 128:256] + t[:, 256:]
                return carry[0] + fold(v), carry[1] + fold(w)

            zero = jnp.zeros((64, 128), F32)
            s1, s2 = lax.fori_loop(0, NB, stat, (zero, zero))
            off = jnp.sum(s1, axis=1, keepdims=True) / D
            var = jnp.sum(s2, axis=1, keepdims=True) / D - off * off
            mean = shift + off
            rstd = lax.rsqrt(jnp.maximum(var, 0.0) + EPS)
            mu[r, :] = mean
            inv[r, :] = rstd

            def put(k, _):
                g = xg[k, pl.ds(0, 1), :].astype(F32)
                unit = (xg[k, r, :].astype(F32) - mean) * rstd
                nrm[r, pl.ds(pl.multiple_of(k * FB, 128), FB)] = (unit * g).astype(BF16)
                return 0

            lax.fori_loop(0, NB, put, 0)

        if img == 0:
            @pl.loop(0, NB)
            def _(k):
                nrm[pl.ds(0, GR), pl.ds(pl.multiple_of(k * FB, 128), FB)] = xg[k, pl.ds(0, GR), :]

    def project(img):
        r = slice(0, GR + IMG) if img == 0 else slice(GR + IMG, ROWS)

        @pl.loop(0, HC // 256)
        def _(c):
            cols = pl.ds(pl.multiple_of(c * 256, 256), 256)
            proj[r, cols] = jnp.dot(nrm[r, :], wv[:, cols], preferred_element_type=F32)

    def transpose(img):
        @pl.loop(0, NB)
        def _(k):
            cols = pl.ds(pl.multiple_of(k * FB, 128), FB)
            rows = slice(GR + img * IMG, GR + (img + 1) * IMG)
            nrm_t[cols, img * IMG:(img + 1) * IMG] = nrm[rows, cols].T

    def head_norm(v):
        cen = v - jnp.mean(v, axis=1, keepdims=True)
        rstd = lax.rsqrt(jnp.mean(cen * cen, axis=1, keepdims=True) + EPS)
        return cen * rstd, rstd

    def norm_back(g, unit, rstd):
        return rstd * (
            g - jnp.mean(g, axis=1, keepdims=True) - unit * jnp.mean(g * unit, axis=1, keepdims=True)
        )

    def attend(img, h):
        r = slice(GR + img * IMG, GR + (img + 1) * IMG)
        rows = slice(img * IMG, (img + 1) * IMG)
        c0 = h * 3 * HEAD_DIM
        cols = [slice(c0 + i * HEAD_DIM, c0 + (i + 1) * HEAD_DIM) for i in range(3)]
        q_gain, k_gain = qkg_ref[h:h + 1, :], qkg_ref[2 + h:3 + h, :]
        q_unit, q_inv = head_norm(proj[r, cols[0]])
        k_unit, k_inv = head_norm(proj[r, cols[1]])
        qn = (q_unit * q_gain).astype(BF16)
        kn = (k_unit * k_gain).astype(BF16)
        v = proj[r, cols[2]].astype(BF16)
        hcols = slice(h * HEAD_DIM, (h + 1) * HEAD_DIM)
        cg = cg_ref[rows, hcols]
        sc = dot_t(qn, kn) * SCALE
        e = jnp.exp(sc - jnp.max(sc, axis=1, keepdims=True))
        probs = e * (1.0 / jnp.sum(e, axis=1, keepdims=True))
        low = probs.astype(BF16)
        ctx_ref[rows, hcols] = jnp.dot(low, v, preferred_element_type=F32).astype(BF16)
        dp = dot_t(cg, v)
        qkvg[rows, cols[2]] = t_dot(low, cg).astype(BF16)
        delta = jnp.sum(probs * dp, axis=1, keepdims=True)
        dsc = (probs * (dp - delta)).astype(BF16)
        dq = jnp.dot(dsc, kn, preferred_element_type=F32) * SCALE
        dk = t_dot(dsc, qn) * SCALE
        for i, (g, unit, rstd, gain) in enumerate(((dq, q_unit, q_inv, q_gain), (dk, k_unit, k_inv, k_gain))):
            part = jnp.sum(g * unit, axis=0, keepdims=True)
            row = slice(1 + 2 * i + h, 2 + 2 * i + h)
            if img > 0:
                part = part + sms[row, :HEAD_DIM]
            sms[row, :HEAD_DIM] = part
            qkvg[rows, cols[i]] = norm_back(g * gain, unit, rstd).astype(BF16)

    def sums(img):
        r = slice(GR + img * IMG, GR + (img + 1) * IMG)
        rows = slice(img * IMG, (img + 1) * IMG)
        g = qkvg[rows, :].astype(F32)
        one = jnp.sum(g * proj[0:1, :], axis=1, keepdims=True)
        two = jnp.sum(g * proj[r, :], axis=1, keepdims=True)
        lane = lax.broadcasted_iota(jnp.int32, (IMG, 128), 1)
        both = jnp.where(lane == 0, one, jnp.where(lane == 1, two, 0.0))
        sxs[:, rows] = both.T[0:8, :]

    sx_copies = []

    def sums_send():
        for o in range(1, NB):
            sx_copies.append(send(sxs, sxr.at[m], {"dp": d, "mp": (m + o) % NB}))

    def sums_end():
        sxr[m] = sxs[...]
        for c in sx_copies:
            c.wait_recv()
        total = sxr[0]
        for k in range(1, NB):
            total = total + sxr[k]
        trans[...] = jnp.zeros_like(trans)
        trans[0:8, :] = total

    cring = {}
    cx = {}

    def term(img, plane, zz):
        b = blk(plane, zz)
        w = wv[pl.ds(pl.multiple_of(b * FB, 16), FB), :]
        return dot_t(qkvg[img * IMG:(img + 1) * IMG, :], w)

    LO, HI = slice(0, HALF), slice(HALF, IMG)
    ORDER = (4, 3, 5, 2, 6, 1, 7, 0)

    def c_plane1(img, o):
        t = term(img, 1, z + o)
        cxs[img, o] = t[LO].astype(BF16)
        cx[(img, o)] = send(cxs.at[img, o], cxr.at[img, o], xh_dev)
        plane1[img, o] = t[HI].astype(BF16)
        if o == 4:
            for i, dr_ in enumerate((1, -1)):
                part = pl.ds(i * HALF // 2, HALF // 2)
                cring[(img, 1, 1, dr_)] = send(
                    plane1.at[img, o, part], t1.at[img, i, 0, part], z_dev[dr_])

    def c_add1(img, s):
        for i, dr_ in enumerate((1, -1)):
            cring[(img, 1, s, dr_)].wait_recv()
            o = (dr_ * (4 - s)) % 8
            mine = plane1[img, o].astype(F32)
            if s == 1:
                a = slice(i * HALF // 2, (i + 1) * HALF // 2)
                b = slice((1 - i) * HALF // 2, (2 - i) * HALF // 2)
                t1[img, i, 0, b] = mine[b].astype(BF16)
                t1[img, i, 0, a] = (mine[a] + t1[img, i, 0, a].astype(F32)).astype(BF16)
            else:
                t1[img, i, s - 1] = (mine + t1[img, i, s - 1].astype(F32)).astype(BF16)
            cring[(img, 1, s + 1, dr_)] = send(t1.at[img, i, s - 1], t1.at[img, i, s], z_dev[dr_])

    def c_end1(img):
        for dr_ in (1, -1):
            cring[(img, 1, 4, dr_)].wait_recv()
        tot = plane1[img, 0].astype(F32) + t1[img, 0, 3].astype(F32) + t1[img, 1, 3].astype(F32)
        cys[img] = tot.astype(BF16)
        cx[(img, "y")] = send(cys.at[img], cyr.at[img], xh_dev)

    def c_start0(img):
        t = term(img, 0, z + 4)
        cx[(img, 4)].wait_recv()
        ci[img, HALF:] = t[HI].astype(BF16)
        ci[img, :HALF] = (t[LO] + cxr[img, 4].astype(F32)).astype(BF16)
        for i, dr_ in enumerate((1, -1)):
            part = pl.ds(i * HALF, HALF)
            cring[(img, 0, 1, dr_)] = send(ci.at[img, part], cr.at[img, i, 0, part], z_dev[dr_])

    def c_add0(img, s):
        for i, dr_ in enumerate((1, -1)):
            o = (dr_ * (4 - s)) % 8
            t = term(img, 0, z + o)
            cx[(img, o)].wait_recv()
            cring[(img, 0, s, dr_)].wait_recv()
            lo = t[LO] + cxr[img, o].astype(F32)
            hi = t[HI]
            if s > 1 or i == 0:
                lo = lo + cr[img, i, s - 1, LO].astype(F32)
            if s > 1 or i == 1:
                hi = hi + cr[img, i, s - 1, HI].astype(F32)
            cr[img, i, s - 1, LO] = lo.astype(BF16)
            cr[img, i, s - 1, HI] = hi.astype(BF16)
            cring[(img, 0, s + 1, dr_)] = send(cr.at[img, i, s - 1], cr.at[img, i, s], z_dev[dr_])

    def c_final(img):
        t = term(img, 0, z)
        cx[(img, 0)].wait_recv()
        for dr_ in (1, -1):
            cring[(img, 0, 4, dr_)].wait_recv()
        cx[(img, "y")].wait_recv()
        ring_sum = cr[img, 0, 3].astype(F32) + cr[img, 1, 3].astype(F32)
        t = t + ring_sum
        lo = t[LO] + cxr[img, 0].astype(F32)
        hi = t[HI] + cyr[img].astype(F32)
        cols = trans[:, img * IMG:(img + 1) * IMG].T
        g = gain_ref[...].astype(F32)
        part = 0.0
        for j, ng in enumerate((lo, hi)):
            r = slice(GR + img * IMG + j * HALF, GR + img * IMG + (j + 1) * HALF)
            c = slice(j * HALF, (j + 1) * HALF)
            rstd = inv[r, :]
            unit = (xg[m, r, :].astype(F32) - mu[r, :]) * rstd
            part = part + jnp.sum(ng * unit, axis=0, keepdims=True)
            back = ng * g
            res = rstd * (back - cols[c, 0:1] / D - unit * (cols[c, 1:2] / D))
            ig_ref[img * IMG + j * HALF:img * IMG + (j + 1) * HALF, :] = res.astype(BF16)
        if img > 0:
            part = part + sms[0:1, :]
        sms[0:1, :] = part

    dcore, dx, dy = {}, {}, {}

    def dest(a, b, same_core):
        xl_ = xl if a == 0 else 1 - xl
        return xl_ * 8 + ((y + b) % 4) * 2 + (core if same_core else 1 - core)

    def wgrad(a, b, same_core):
        k = dest(a, b, same_core)
        return jnp.dot(nrm_t[pl.ds(pl.multiple_of(k * FB, 16), FB), :], qkvg[...], preferred_element_type=F32)

    def d_core(a, b):
        j = a * 4 + b
        ds[j] = wgrad(a, b, False).astype(BF16)
        dcore[j] = send(ds.at[j], dr.at[j], core_dev)

    XS, YS = pl.ds(0, XC), pl.ds(XC, HC - XC)

    def y_start(key, ref, cols):
        for i, dr_ in enumerate((1, -1)):
            part = pl.ds(i * FB // 2, FB // 2)
            dy[(key, 1, dr_)] = send(ref.at[part, cols], dyr.at[key, i, 0, part], y_dev[dr_])

    def d_own1(b):
        g = wgrad(1, b, True)
        j = 4 + b
        dcore[j].wait_recv()
        dr[j] = (g + dr[j].astype(F32)).astype(BF16)
        dx[b] = send(dr.at[j, :, XS], dxr.at[b], xl_dev)
        if b == 2:
            y_start(1, dr.at[j], YS)

    def d_own0(b):
        g = wgrad(0, b, True)
        dcore[b].wait_recv()
        tot = g + dr[b].astype(F32)
        dx[b].wait_recv()
        dr[b, :, XC:] = tot[:, XC:].astype(BF16)
        dr[b, :, :XC] = (tot[:, :XC] + dxr[b].astype(F32)).astype(BF16)
        if b == 2:
            y_start(2, dr.at[b], YS)
            y_start(0, dr.at[b], XS)

    def d_mid(key):
        cols = slice(0, XC) if key == 0 else slice(XC, HC)
        cds = XS if key == 0 else YS
        for i, dr_ in enumerate((1, -1)):
            j = (4 if key == 1 else 0) + (1 if i == 0 else 3)
            dy[(key, 1, dr_)].wait_recv()
            part = slice(i * FB // 2, (i + 1) * FB // 2)
            dr[j, part, cols] = (dr[j, part, cols].astype(F32) + dyr[key, i, 0, part].astype(F32)).astype(BF16)
            dy[(key, 2, dr_)] = send(dr.at[j, :, cds], dyr.at[key, i, 1], y_dev[dr_])

    def d_last(key):
        cols = slice(0, XC) if key == 0 else slice(XC, HC)
        for dr_ in (1, -1):
            dy[(key, 2, dr_)].wait_recv()
        j = 4 if key == 1 else 0
        tot = dr[j, :, cols].astype(F32) + dyr[key, 0, 1].astype(F32) + dyr[key, 1, 1].astype(F32)
        if key == 1:
            dr[j, :, cols] = tot.astype(BF16)
            dx["l"] = send(dr.at[j, :, cds_y], dxl, xl_dev)
        elif key == 0:
            wg_ref[:, cols] = tot.astype(BF16)
        else:
            dx["l"].wait_recv()
            wg_ref[:, cols] = (tot + dxl[...].astype(F32)).astype(BF16)

    cds_y = YS

    ag0(0)
    ag0(1)
    ag1(0)
    ag1(1)
    weights.wait()
    for s in (1, 2, 3, 4):
        for img in (0, 1):
            for plane in (0, 1):
                ag_hop(img, plane, s)
    ag_end(0)
    sms[...] = jnp.zeros_like(sms)
    norm(0)
    project(0)
    ag_end(1)
    attend(0, 0)
    attend(0, 1)
    sums(0)
    for o in ORDER:
        c_plane1(0, o)
    c_start0(0)
    norm(1)
    project(1)
    c_add1(0, 1)
    c_add0(0, 1)
    attend(1, 0)
    c_add1(0, 2)
    c_add0(0, 2)
    attend(1, 1)
    sums(1)
    sums_send()
    c_add1(0, 3)
    c_add0(0, 3)
    for o in ORDER:
        c_plane1(1, o)
    c_start0(1)
    transpose(0)
    transpose(1)
    for a in (1, 0):
        for b in (2, 1, 3, 0):
            d_core(a, b)
    c_end1(0)
    for b in (2, 1, 3, 0):
        d_own1(b)
    c_add1(1, 1)
    c_add0(1, 1)
    sums_end()
    c_final(0)
    d_own0(2)
    d_mid(1)
    d_own0(1)
    d_own0(3)
    d_own0(0)
    c_add1(1, 2)
    c_add0(1, 2)
    d_last(1)
    d_mid(2)
    d_mid(0)
    c_add1(1, 3)
    c_add0(1, 3)
    d_last(0)
    c_end1(1)
    c_final(1)
    sm_copies = []
    for o in range(1, NB):
        sm_copies.append(send(sms, smr.at[d], {"dp": (d + o) % NB, "mp": m}))
    smr[d] = sms[...]
    d_last(2)
    for c in sm_copies:
        c.wait_recv()
    total = smr[0]
    for k in range(1, NB):
        total = total + smr[k]
    small_ref[...] = total
    for c in sends:
        c.wait_send()


def per_device(patches, norm_gain, qkv_weight, qk_gain, context_grad):
    vmem = pl.BlockSpec(memory_space=pltpu.VMEM)
    hbm = pl.BlockSpec(memory_space=pl.ANY)
    flops = 2 * TOK * D * HC * 3
    ctx, ig, wg, small = pl.pallas_call(
        kernel,
        out_shape=(
            jax.ShapeDtypeStruct((TOK, 256), BF16),
            jax.ShapeDtypeStruct((TOK, FB), BF16),
            jax.ShapeDtypeStruct((FB, HC), BF16),
            jax.ShapeDtypeStruct((8, FB), F32),
        ),
        in_specs=[hbm, vmem, hbm, vmem, vmem],
        out_specs=(vmem, vmem, vmem, vmem),
        scratch_shapes=[
            pltpu.VMEM((NB, ROWS, FB), BF16),
            pltpu.VMEM((D, HC), BF16),
            pltpu.VMEM((ROWS, D), BF16),
            pltpu.VMEM((D, TOK), BF16),
            pltpu.VMEM((ROWS, HC), F32),
            pltpu.VMEM((TOK, HC), BF16),
            pltpu.VMEM((ROWS, 1), F32),
            pltpu.VMEM((ROWS, 1), F32),
            pltpu.VMEM((NIMG, 2, 4, IMG, FB), BF16),
            pltpu.VMEM((NIMG, IMG, FB), BF16),
            pltpu.VMEM((NIMG, 2, 4, HALF, FB), BF16),
            pltpu.VMEM((NIMG, 8, HALF, FB), BF16),
            pltpu.VMEM((NIMG, 8, HALF, FB), BF16),
            pltpu.VMEM((NIMG, HALF, FB), BF16),
            pltpu.VMEM((NIMG, HALF, FB), BF16),
            pltpu.VMEM((NIMG, 8, HALF, FB), BF16),
            pltpu.VMEM((8, FB, HC), BF16),
            pltpu.VMEM((8, FB, HC), BF16),
            pltpu.VMEM((4, FB, XC), BF16),
            pltpu.VMEM((FB, HC - XC), BF16),
            pltpu.VMEM((3, 2, 2, FB, XC), BF16),
            pltpu.VMEM((8, TOK), F32),
            pltpu.VMEM((NB, 8, TOK), F32),
            pltpu.VMEM((128, TOK), F32),
            pltpu.VMEM((8, FB), F32),
            pltpu.VMEM((NB, 8, FB), F32),
            pltpu.SemaphoreType.DMA((NSEM,)),
            pltpu.SemaphoreType.DMA((NSEM,)),
            pltpu.SemaphoreType.DMA((2,)),
        ],
        compiler_params=pltpu.CompilerParams(
            collective_id=0, has_side_effects=True, vmem_limit_bytes=62 * 2**20
        ),
        cost_estimate=pl.CostEstimate(flops=flops, bytes_accessed=2**25, transcendentals=2**18),
    )(patches, norm_gain.reshape(1, FB), qkv_weight, qk_gain.reshape(4, HEAD_DIM), context_grad)
    return ctx, ig, wg, small[0], small[1:5, :HEAD_DIM].reshape(2, 2, HEAD_DIM)


def solution(mesh):
    in_specs = (P("dp", "mp"), P("mp"), P(None, "mp"), P(None, "mp", None), P("dp", "mp"))
    out_specs = (P("dp", "mp"), P("dp", "mp"), P("dp", "mp"), P("mp"), P(None, "mp", None))
    return jax.shard_map(
        per_device, mesh=mesh, in_specs=in_specs, out_specs=out_specs, check_vma=False
    )
```

```python
import functools
import math

import jax
import jax.numpy as jnp
from jax import lax
from jax.experimental import pallas as pl
from jax.experimental.pallas import tpu as pltpu
from jax.sharding import PartitionSpec as P

HEAD_DIM = 128
IMG = 256
NIMG = 2
TOK = IMG * NIMG
FB = 384
NB = 16
D = FB * NB
HC = 768
GR = 16
ROWS = GR + TOK
HALF = IMG // 2
BASE = (0, IMG + GR)
XC = 256
LOW = (128, 64)
EPS = 1e-6
SCALE = 1.0 / math.sqrt(HEAD_DIM)
MESH = pl.DeviceIdType.MESH
F32 = jnp.float32
BF16 = jnp.bfloat16
NSEM = 192


def dot_t(a, b):
    return lax.dot_general(a, b, (((1,), (1,)), ((), ())), preferred_element_type=F32)


def t_dot(a, b):
    return lax.dot_general(a, b, (((0,), (0,)), ((), ())), preferred_element_type=F32)


def kernel(
    p_hbm, gain_ref, w_hbm, qkg_ref, cg_ref,
    ctx_ref, ig_ref, wg_ref, small_ref,
    xg, wv, nrm, nrm_t, proj, qkvg, mu, inv,
    cr, ci, ci1, t1, cxs_a, cxs_b, cxr_a, cxr_b, plane1_a, plane1_b, cys, cyr,
    ds, dr, dxr, dxl, dyx, dyy,
    sxs, sxr, trans, sms, smr,
    ss, rs, ls,
):
    d = lax.axis_index("dp")
    m = lax.axis_index("mp")
    xl, y, core = d // 8, (d // 2) % 4, d % 2
    xh, z = m // 8, m % 8
    count = [0]
    sends = []

    def at(xl_=None, y_=None, core_=None, xh_=None, z_=None):
        xl_ = xl if xl_ is None else xl_
        y_ = y if y_ is None else y_
        core_ = core if core_ is None else core_
        xh_ = xh if xh_ is None else xh_
        z_ = z if z_ is None else z_
        return {"dp": xl_ * 8 + y_ * 2 + core_, "mp": xh_ * 8 + z_}

    z_dev = {1: at(z_=(z + 1) % 8), -1: at(z_=(z + 7) % 8)}
    y_dev = {1: at(y_=(y + 1) % 4), -1: at(y_=(y + 3) % 4)}
    xh_dev = at(xh_=1 - xh)
    xl_dev = at(xl_=1 - xl)
    core_dev = at(core_=1 - core)

    def send(src, dst, dev):
        i = count[0]
        count[0] += 1
        copy = pltpu.make_async_remote_copy(
            src_ref=src, dst_ref=dst, send_sem=ss.at[i], recv_sem=rs.at[i],
            device_id=dev, device_id_type=MESH,
        )
        copy.start()
        sends.append(copy)
        return copy

    own = [
        pltpu.make_async_copy(
            p_hbm.at[pl.ds(i * IMG, IMG)], xg.at[m, pl.ds(BASE[i], IMG)], ls.at[i])
        for i in range(NIMG)
    ]
    for c in own:
        c.start()
    weights = pltpu.make_async_copy(w_hbm, wv, ls.at[2])
    weights.start()
    gain = gain_ref[...].reshape(1, FB)
    xg[m, pl.ds(IMG, GR), :] = jnp.broadcast_to(gain, (GR, FB))
    barrier = pltpu.get_barrier_semaphore()
    for o in range(1, NB):
        pl.semaphore_signal(barrier, inc=1, device_id={"dp": d, "mp": (m + o) % NB}, device_id_type=MESH)
        pl.semaphore_signal(barrier, inc=1, device_id={"dp": (d + o) % NB, "mp": m}, device_id_type=MESH)
    pl.semaphore_wait(barrier, 2 * (NB - 1))
    for c in own:
        c.wait()

    def blk(plane, zz):
        return (xh if plane == 0 else 1 - xh) * 8 + (zz + 16) % 8

    def span(img, part):
        lo0 = BASE[img]
        mid = lo0 + HALF
        end = lo0 + IMG + (GR if img == 0 else 0)
        return {
            "full": (lo0, end - lo0),
            "lo": (lo0, mid - lo0),
            "hi": (mid, end - mid),
            "hi0": (mid, HALF // 2),
            "hi1": (mid + HALF // 2, end - mid - HALF // 2),
        }[part]

    ring = {}
    xrecv = {0: [], 1: []}

    def send_block(img, plane, origin_z, part, dev):
        r, n = span(img, part)
        ref = xg.at[blk(plane, origin_z), pl.ds(r, n)]
        return send(ref, ref, dev)

    def hop_parts(plane):
        if plane == 0:
            return {1: "full", -1: "full"}, {1: "lo", -1: "hi"}
        return {1: "hi", -1: "hi"}, {1: "hi0", -1: "hi1"}

    def forward(img, plane, s):
        parts = hop_parts(plane)[0 if s < 4 else 1]
        for dr_ in (1, -1):
            ring[(img, plane, s, dr_)] = send_block(img, plane, z - (s - 1) * dr_, parts[dr_], z_dev[dr_])

    def arrive(img, plane, s):
        for dr_ in (1, -1):
            ring[(img, plane, s, dr_)].wait_recv()

    def ag0(img):
        ring[(img, "x")] = send_block(img, 0, z, "hi", xh_dev)
        forward(img, 0, 1)
        xrecv[img].append(send_block(img, 0, z, "lo", xh_dev))

    def ag1(img):
        ring[(img, "x")].wait_recv()
        forward(img, 1, 1)

    def ag_hop(img, plane, s):
        arrive(img, plane, s)
        if s < 4:
            forward(img, plane, s + 1)
        if plane == 0:
            for dr_ in (1, -1) if s < 4 else (1,):
                xrecv[img].append(send_block(img, 0, z - s * dr_, "lo", xh_dev))

    def ag_end(img):
        for c in xrecv[img]:
            c.wait_recv()

    def norm(img, half):
        @pl.loop(0, HALF // 64)
        def _(c):
            r = pl.ds(pl.multiple_of(BASE[img] + half * HALF + c * 64, 16), 64)
            shift = jnp.mean(xg[0, r, :].astype(F32), axis=1, keepdims=True)

            def stat(k, carry):
                v = xg[k, r, :].astype(F32) - shift
                w = v * v
                fold = lambda t: t[:, :128] + t[:, 128:256] + t[:, 256:]
                return carry[0] + fold(v), carry[1] + fold(w)

            zero = jnp.zeros((64, 128), F32)
            s1, s2 = lax.fori_loop(0, NB, stat, (zero, zero))
            off = jnp.sum(s1, axis=1, keepdims=True) / D
            var = jnp.sum(s2, axis=1, keepdims=True) / D - off * off
            mean = shift + off
            rstd = lax.rsqrt(jnp.maximum(var, 0.0) + EPS)
            mu[r, :] = mean
            inv[r, :] = rstd

            def put(k, _):
                g = xg[k, pl.ds(IMG, 1), :].astype(F32)
                unit = (xg[k, r, :].astype(F32) - mean) * rstd
                nrm[r, pl.ds(pl.multiple_of(k * FB, 128), FB)] = (unit * g).astype(BF16)
                return 0

            lax.fori_loop(0, NB, put, 0)

        if img == 0 and half == 1:
            @pl.loop(0, NB)
            def _(k):
                nrm[pl.ds(IMG, GR), pl.ds(pl.multiple_of(k * FB, 128), FB)] = xg[k, pl.ds(IMG, GR), :]

    def project(img):
        r = slice(0, BASE[1]) if img == 0 else slice(BASE[1], ROWS)

        @pl.loop(0, HC // 256)
        def _(c):
            cols = pl.ds(pl.multiple_of(c * 256, 256), 256)
            proj[r, cols] = jnp.dot(nrm[r, :], wv[:, cols], preferred_element_type=F32)

    def transpose(img):
        @pl.loop(0, NB)
        def _(k):
            cols = pl.ds(pl.multiple_of(k * FB, 128), FB)
            rows = slice(BASE[img], BASE[img] + IMG)
            nrm_t[cols, img * IMG:(img + 1) * IMG] = nrm[rows, cols].T

    def head_norm(v):
        cen = v - jnp.mean(v, axis=1, keepdims=True)
        rstd = lax.rsqrt(jnp.mean(cen * cen, axis=1, keepdims=True) + EPS)
        return cen * rstd, rstd

    def norm_back(g, unit, rstd):
        return rstd * (
            g - jnp.mean(g, axis=1, keepdims=True) - unit * jnp.mean(g * unit, axis=1, keepdims=True)
        )

    def attend(img, h):
        r = slice(BASE[img], BASE[img] + IMG)
        rows = slice(img * IMG, (img + 1) * IMG)
        c0 = h * 3 * HEAD_DIM
        cols = [slice(c0 + i * HEAD_DIM, c0 + (i + 1) * HEAD_DIM) for i in range(3)]
        q_gain, k_gain = qkg_ref[0, h:h + 1, :], qkg_ref[1, h:h + 1, :]
        q_unit, q_inv = head_norm(proj[r, cols[0]])
        k_unit, k_inv = head_norm(proj[r, cols[1]])
        qn = (q_unit * q_gain).astype(BF16)
        kn = (k_unit * k_gain).astype(BF16)
        v = proj[r, cols[2]].astype(BF16)
        hcols = slice(h * HEAD_DIM, (h + 1) * HEAD_DIM)
        cg = cg_ref[rows, hcols]
        sc = dot_t(qn, kn) * SCALE
        e = jnp.exp(sc - jnp.max(sc, axis=1, keepdims=True))
        probs = e * (1.0 / jnp.sum(e, axis=1, keepdims=True))
        low = probs.astype(BF16)
        ctx_ref[rows, hcols] = jnp.dot(low, v, preferred_element_type=F32).astype(BF16)
        dp = dot_t(cg, v)
        qkvg[rows, cols[2]] = t_dot(low, cg).astype(BF16)
        delta = jnp.sum(probs * dp, axis=1, keepdims=True)
        dsc = (probs * (dp - delta)).astype(BF16)
        dq = jnp.dot(dsc, kn, preferred_element_type=F32) * SCALE
        dk = t_dot(dsc, qn) * SCALE
        for i, (g, unit, rstd, gain) in enumerate(((dq, q_unit, q_inv, q_gain), (dk, k_unit, k_inv, k_gain))):
            part = jnp.sum(g * unit, axis=0, keepdims=True)
            row = slice(3 + 2 * i + h, 4 + 2 * i + h)
            if img > 0:
                part = part + sms[row, :]
            sms[row, :] = part
            qkvg[rows, cols[i]] = norm_back(g * gain, unit, rstd).astype(BF16)

    def sums(img):
        r = slice(BASE[img], BASE[img] + IMG)
        rows = slice(img * IMG, (img + 1) * IMG)
        g = qkvg[rows, :].astype(F32)
        one = jnp.sum(g * proj[IMG:IMG + 1, :], axis=1, keepdims=True)
        two = jnp.sum(g * proj[r, :], axis=1, keepdims=True)
        lane = lax.broadcasted_iota(jnp.int32, (IMG, 128), 1)
        both = jnp.where(lane == 0, one, jnp.where(lane == 1, two, 0.0))
        turned = both.T
        for i in range(2):
            for j in range(2):
                row = img * 4 + i * 2 + j
                sxs[row:row + 1, :] = turned[i:i + 1, j * 128:(j + 1) * 128]

    sx_copies = []

    def sums_send():
        for o in range(1, NB):
            sx_copies.append(send(sxs, sxr.at[m], {"dp": d, "mp": (m + o) % NB}))

    def sums_end():
        sxr[m] = sxs[...]
        for c in sx_copies:
            c.wait_recv()
        total = sxr[0]
        for k in range(1, NB):
            total = total + sxr[k]
        trans[...] = jnp.zeros_like(trans)
        for row in range(8):
            i, c = (row // 2) % 2, (row // 4) * IMG + (row % 2) * 128
            trans[i:i + 1, c:c + 128] = total[row:row + 1, :]

    cring = {}
    cx = {}

    def term(img, plane, zz):
        b = blk(plane, zz)
        w = wv[pl.ds(pl.multiple_of(b * FB, 16), FB), :]
        return dot_t(qkvg[img * IMG:(img + 1) * IMG, :], w)

    cxs, cxr, plane1 = (cxs_a, cxs_b), (cxr_a, cxr_b), (plane1_a, plane1_b)
    ORDER = (4, 3, 5, 2, 6, 1, 7, 0)

    def c_plane1(img, o):
        n = LOW[img]
        t = term(img, 1, z + o)
        cxs[img][o] = t[:n].astype(BF16)
        cx[(img, o)] = send(cxs[img].at[o], cxr[img].at[o], xh_dev)
        plane1[img][o] = t[n:].astype(BF16)

    def high(img, o):
        return plane1[img][o].astype(F32) if LOW[img] else term(img, 1, z + o)

    def c_start1(img):
        n = IMG - LOW[img]
        ci1[img, :n] = high(img, 4).astype(BF16)
        for i, dr_ in enumerate((1, -1)):
            part = pl.ds(i * n // 2, n // 2)
            cring[(img, 1, 1, dr_)] = send(ci1.at[img, part], t1.at[img, i, 0, part], z_dev[dr_])

    def c_add1(img, s):
        n = IMG - LOW[img]
        rows = pl.ds(0, n)
        for i, dr_ in enumerate((1, -1)):
            mine = high(img, (dr_ * (4 - s)) % 8)
            cring[(img, 1, s, dr_)].wait_recv()
            if s == 1:
                a = slice(i * n // 2, (i + 1) * n // 2)
                b = slice((1 - i) * n // 2, (2 - i) * n // 2)
                t1[img, i, 0, b] = mine[b].astype(BF16)
                t1[img, i, 0, a] = (mine[a] + t1[img, i, 0, a].astype(F32)).astype(BF16)
            else:
                t1[img, i, s - 1, :n] = (mine + t1[img, i, s - 1, :n].astype(F32)).astype(BF16)
            cring[(img, 1, s + 1, dr_)] = send(
                t1.at[img, i, s - 1, rows], t1.at[img, i, s, rows], z_dev[dr_])

    def c_end1(img):
        n = IMG - LOW[img]
        mine = high(img, 0)
        for dr_ in (1, -1):
            cring[(img, 1, 4, dr_)].wait_recv()
        tot = mine + t1[img, 0, 3, :n].astype(F32) + t1[img, 1, 3, :n].astype(F32)
        cys[img, :n] = tot.astype(BF16)
        cx[(img, "y")] = send(cys.at[img, pl.ds(0, n)], cyr.at[img, pl.ds(0, n)], xh_dev)

    def from_x(img, o):
        t = term(img, 0, z + o)
        n = LOW[img]
        if not n:
            return t
        cx[(img, o)].wait_recv()
        return jnp.concatenate([t[:n] + cxr[img][o].astype(F32), t[n:]], axis=0)

    def c_start0(img):
        ci[img] = from_x(img, 4).astype(BF16)
        for i, dr_ in enumerate((1, -1)):
            part = pl.ds(i * HALF, HALF)
            cring[(img, 0, 1, dr_)] = send(ci.at[img, part], cr.at[img, i, 0, part], z_dev[dr_])

    def c_add0(img, s):
        for i, dr_ in enumerate((1, -1)):
            t = from_x(img, (dr_ * (4 - s)) % 8)
            cring[(img, 0, s, dr_)].wait_recv()
            if s == 1:
                a, b = slice(i * HALF, (i + 1) * HALF), slice((1 - i) * HALF, (2 - i) * HALF)
                cr[img, i, 0, b] = t[b].astype(BF16)
                cr[img, i, 0, a] = (t[a] + cr[img, i, 0, a].astype(F32)).astype(BF16)
            else:
                cr[img, i, s - 1] = (t + cr[img, i, s - 1].astype(F32)).astype(BF16)
            cring[(img, 0, s + 1, dr_)] = send(cr.at[img, i, s - 1], cr.at[img, i, s], z_dev[dr_])

    def c_final(img):
        n = LOW[img]
        t = from_x(img, 0)
        for dr_ in (1, -1):
            cring[(img, 0, 4, dr_)].wait_recv()
        t = t + cr[img, 0, 3].astype(F32) + cr[img, 1, 3].astype(F32)
        cx[(img, "y")].wait_recv()
        rest = t[n:] + cyr[img, :IMG - n].astype(F32)
        ng = jnp.concatenate([t[:n], rest], axis=0) if n else rest
        cols = trans[:, img * IMG:(img + 1) * IMG].T
        r = slice(BASE[img], BASE[img] + IMG)
        rstd = inv[r, :]
        unit = (xg[m, r, :].astype(F32) - mu[r, :]) * rstd
        part = jnp.sum(ng * unit, axis=0, keepdims=True)
        back = ng * gain.astype(F32)
        res = rstd * (back - cols[:, 0:1] / D - unit * (cols[:, 1:2] / D))
        ig_ref[img * IMG:(img + 1) * IMG, :] = res.astype(BF16)
        for i in range(3):
            sms[i:i + 1, :] = sms[i:i + 1, :] + part[:, i * 128:(i + 1) * 128]

    dcore, dx, dy = {}, {}, {}

    def dest(a, b, same_core):
        xl_ = xl if a == 0 else 1 - xl
        return xl_ * 8 + ((y + b) % 4) * 2 + (core if same_core else 1 - core)

    def wgrad(a, b, same_core):
        k = dest(a, b, same_core)
        return jnp.dot(nrm_t[pl.ds(pl.multiple_of(k * FB, 16), FB), :], qkvg[...], preferred_element_type=F32)

    def d_core(a, b):
        j = a * 4 + b
        ds[j] = wgrad(a, b, False).astype(BF16)
        dcore[j] = send(ds.at[j], dr.at[j], core_dev)

    XS, YS = pl.ds(0, XC), pl.ds(XC, HC - XC)

    def y_buf(key):
        return dyx if key == 0 else dyy.at[key - 1]

    def y_start(key, ref, cols):
        for i, dr_ in enumerate((1, -1)):
            part = pl.ds(i * FB // 2, FB // 2)
            dy[(key, 1, dr_)] = send(ref.at[part, cols], y_buf(key).at[i, 0, part], y_dev[dr_])

    def d_own1(b):
        g = wgrad(1, b, True)
        j = 4 + b
        dcore[j].wait_recv()
        dr[j] = (g + dr[j].astype(F32)).astype(BF16)
        dx[b] = send(dr.at[j, :, XS], dxr.at[b], xl_dev)
        if b == 2:
            y_start(1, dr.at[j], YS)

    def d_own0(b):
        g = wgrad(0, b, True)
        dcore[b].wait_recv()
        dr[b] = (g + dr[b].astype(F32)).astype(BF16)
        if b == 2:
            y_start(2, dr.at[b], YS)

    def d_x0(b):
        dx[b].wait_recv()
        dr[b, :, :XC] = (dr[b, :, :XC].astype(F32) + dxr[b].astype(F32)).astype(BF16)
        if b == 2:
            y_start(0, dr.at[b], XS)

    def d_mid(key):
        cols = slice(0, XC) if key == 0 else slice(XC, HC)
        cds = XS if key == 0 else YS
        buf = y_buf(key)
        for i, dr_ in enumerate((1, -1)):
            j = (4 if key == 1 else 0) + (1 if i == 0 else 3)
            dy[(key, 1, dr_)].wait_recv()
            part = slice(i * FB // 2, (i + 1) * FB // 2)
            dr[j, part, cols] = (dr[j, part, cols].astype(F32) + buf[i, 0, part].astype(F32)).astype(BF16)
            dy[(key, 2, dr_)] = send(dr.at[j, :, cds], buf.at[i, 1], y_dev[dr_])

    def d_last(key):
        cols = slice(0, XC) if key == 0 else slice(XC, HC)
        buf = y_buf(key)
        for dr_ in (1, -1):
            dy[(key, 2, dr_)].wait_recv()
        j = 4 if key == 1 else 0
        tot = dr[j, :, cols].astype(F32) + buf[0, 1].astype(F32) + buf[1, 1].astype(F32)
        if key == 1:
            dr[j, :, cols] = tot.astype(BF16)
            dx["l"] = send(dr.at[j, :, YS], dxl, xl_dev)
        elif key == 0:
            wg_ref[:, cols] = tot.astype(BF16)
        else:
            dx["l"].wait_recv()
            wg_ref[:, cols] = (tot + dxl[...].astype(F32)).astype(BF16)

    def sums_start():
        sms[...] = jnp.zeros_like(sms)

    def small_send():
        for o in range(1, NB):
            sm_copies.append(send(sms, smr.at[d], {"dp": (d + o) % NB, "mp": m}))
        smr[d] = sms[...]

    def small_end():
        for c in sm_copies:
            c.wait_recv()
        total = smr[0]
        for k in range(1, NB):
            total = total + smr[k]
        small_ref[...] = total

    sm_copies = []
    steps = []

    def do(f, *a):
        steps.append((f, a))

    do(ag0, 0)
    do(ag0, 1)
    do(weights.wait)
    do(ag_hop, 0, 0, 1)
    do(sums_start)
    do(ag1, 0)
    do(ag_hop, 0, 0, 2)
    do(ag_hop, 0, 1, 1)
    do(ag_hop, 0, 0, 3)
    do(ag_hop, 0, 1, 2)
    do(ag_hop, 1, 0, 1)
    do(ag_hop, 0, 1, 3)
    do(ag1, 1)
    do(ag_hop, 0, 0, 4)
    do(ag_hop, 1, 0, 2)
    do(ag_hop, 0, 1, 4)
    do(norm, 0, 1)
    do(ag_hop, 1, 1, 1)
    do(ag_end, 0)
    do(norm, 0, 0)
    do(project, 0)
    do(ag_hop, 1, 0, 3)
    do(attend, 0, 0)
    do(ag_hop, 1, 1, 2)
    do(attend, 0, 1)
    do(c_plane1, 0, 4)
    do(c_start1, 0)
    do(ag_hop, 1, 0, 4)
    do(c_plane1, 0, 5)
    do(transpose, 0)
    do(ag_hop, 1, 1, 3)
    do(sums, 0)
    do(c_plane1, 0, 3)
    do(c_add1, 0, 1)
    do(c_plane1, 0, 7)
    do(c_plane1, 0, 1)
    do(c_plane1, 0, 6)
    do(c_start0, 0)
    do(ag_hop, 1, 1, 4)
    do(norm, 1, 1)
    do(c_plane1, 0, 2)
    do(c_add1, 0, 2)
    do(ag_end, 1)
    do(norm, 1, 0)
    do(project, 1)
    do(c_add1, 0, 3)
    do(c_add0, 0, 1)
    do(attend, 1, 0)
    do(attend, 1, 1)
    do(c_plane1, 1, 4)
    do(c_start1, 1)
    do(sums, 1)
    do(c_plane1, 1, 5)
    do(c_plane1, 1, 0)
    do(transpose, 1)
    do(d_core, 1, 2)
    do(c_plane1, 1, 1)
    do(sums_send)
    do(c_start0, 1)
    do(d_core, 1, 3)
    do(c_plane1, 1, 2)
    do(c_plane1, 1, 3)
    do(c_add1, 1, 1)
    do(d_own1, 2)
    do(d_core, 0, 1)
    do(d_core, 0, 2)
    do(c_add0, 0, 2)
    do(c_plane1, 1, 7)
    do(d_own1, 3)
    do(c_add0, 1, 1)
    do(d_core, 1, 1)
    do(d_own0, 2)
    do(d_x0, 2)
    do(d_core, 0, 3)
    do(c_plane1, 1, 6)
    do(d_own1, 1)
    do(d_mid, 1)
    do(c_plane1, 0, 0)
    do(d_core, 1, 0)
    do(c_add1, 1, 2)
    do(c_end1, 0)
    do(d_own0, 3)
    do(c_add0, 1, 2)
    do(sums_end)
    do(d_own1, 0)
    do(d_x0, 3)
    do(d_own0, 1)
    do(d_x0, 1)
    do(c_add1, 1, 3)
    do(d_core, 0, 0)
    do(c_add0, 0, 3)
    do(d_mid, 0)
    do(c_add0, 1, 3)
    do(d_mid, 2)
    do(c_end1, 1)
    do(d_last, 1)
    do(c_final, 0)
    do(d_own0, 0)
    do(d_x0, 0)
    do(d_last, 0)
    do(c_final, 1)
    do(small_send)
    do(small_end)
    do(d_last, 2)
    for f, a in steps:
        f(*a)
    for c in sends:
        c.wait_send()


def place(ctx, ig, wg, small, ctx_out, ig_out, wg_out, ngg_out, qkg_out):
    ctx_out[...] = ctx[...]
    ig_out[...] = ig[...]
    wg_out[...] = wg[...]
    for i in range(3):
        ngg_out[pl.ds(i * 128, 128)] = small[i, :]
    for i in range(2):
        qkg_out[i] = small[3 + 2 * i:5 + 2 * i, :]


def per_device(patches, norm_gain, qkv_weight, qk_gain, context_grad):
    vmem = pl.BlockSpec(memory_space=pltpu.VMEM)
    hbm = pl.BlockSpec(memory_space=pl.ANY)
    flops = 2 * TOK * D * HC * 3
    ctx, ig, wg, small = pl.pallas_call(
        kernel,
        out_shape=(
            jax.ShapeDtypeStruct((TOK, 256), BF16),
            jax.ShapeDtypeStruct((TOK, FB), BF16),
            jax.ShapeDtypeStruct((FB, HC), BF16),
            jax.ShapeDtypeStruct((8, 128), F32),
        ),
        in_specs=[hbm, vmem, hbm, vmem, vmem],
        out_specs=(vmem, vmem, vmem, vmem),
        scratch_shapes=[
            pltpu.VMEM((NB, ROWS, FB), BF16),
            pltpu.VMEM((D, HC), BF16),
            pltpu.VMEM((ROWS, D), BF16),
            pltpu.VMEM((D, TOK), BF16),
            pltpu.VMEM((ROWS, HC), F32),
            pltpu.VMEM((TOK, HC), BF16),
            pltpu.VMEM((ROWS, 1), F32),
            pltpu.VMEM((ROWS, 1), F32),
            pltpu.VMEM((NIMG, 2, 4, IMG, FB), BF16),
            pltpu.VMEM((NIMG, IMG, FB), BF16),
            pltpu.VMEM((NIMG, IMG, FB), BF16),
            pltpu.VMEM((NIMG, 2, 4, IMG, FB), BF16),
            *[pltpu.VMEM((8, max(n, 16), FB), BF16) for n in LOW],
            *[pltpu.VMEM((8, max(n, 16), FB), BF16) for n in LOW],
            *[pltpu.VMEM((8, IMG - n if n else 16, FB), BF16) for n in LOW],
            pltpu.VMEM((NIMG, IMG, FB), BF16),
            pltpu.VMEM((NIMG, IMG, FB), BF16),
            pltpu.VMEM((8, FB, HC), BF16),
            pltpu.VMEM((8, FB, HC), BF16),
            pltpu.VMEM((4, FB, XC), BF16),
            pltpu.VMEM((FB, HC - XC), BF16),
            pltpu.VMEM((2, 2, FB, XC), BF16),
            pltpu.VMEM((2, 2, 2, FB, HC - XC), BF16),
            pltpu.VMEM((8, 128), F32),
            pltpu.VMEM((NB, 8, 128), F32),
            pltpu.VMEM((128, TOK), F32),
            pltpu.VMEM((8, 128), F32),
            pltpu.VMEM((NB, 8, 128), F32),
            pltpu.SemaphoreType.DMA((NSEM,)),
            pltpu.SemaphoreType.DMA((NSEM,)),
            pltpu.SemaphoreType.DMA((3,)),
        ],
        compiler_params=pltpu.CompilerParams(
            collective_id=0, has_side_effects=True, vmem_limit_bytes=62 * 2**20
        ),
        cost_estimate=pl.CostEstimate(flops=flops, bytes_accessed=2**25, transcendentals=2**18),
    )(patches, norm_gain, qkv_weight, qk_gain, context_grad)
    return pl.pallas_call(
        place,
        out_shape=(
            jax.ShapeDtypeStruct((TOK, 256), BF16),
            jax.ShapeDtypeStruct((TOK, FB), BF16),
            jax.ShapeDtypeStruct((FB, HC), BF16),
            jax.ShapeDtypeStruct((FB,), F32),
            jax.ShapeDtypeStruct((2, 2, HEAD_DIM), F32),
        ),
        in_specs=[vmem] * 4,
        out_specs=(vmem,) * 5,
    )(ctx, ig, wg, small)


def solution(mesh):
    in_specs = (P("dp", "mp"), P("mp"), P(None, "mp"), P(None, "mp", None), P("dp", "mp"))
    out_specs = (P("dp", "mp"), P("dp", "mp"), P("dp", "mp"), P("mp"), P(None, "mp", None))
    return jax.shard_map(
        per_device, mesh=mesh, in_specs=in_specs, out_specs=out_specs, check_vma=False
    )
```

```python
import functools
import math

import jax
import jax.numpy as jnp
from jax import lax
from jax.experimental import pallas as pl
from jax.experimental.pallas import tpu as pltpu
from jax.sharding import PartitionSpec as P

HEAD_DIM = 128
IMG = 256
NIMG = 2
TOK = IMG * NIMG
FB = 384
NB = 16
D = FB * NB
HC = 768
GR = 16
ROWS = GR + TOK
HALF = IMG // 2
BASE = (0, IMG + GR)
XC = 128
LOW = (96, 96)
EPS = 1e-6
SCALE = 1.0 / math.sqrt(HEAD_DIM)
MESH = pl.DeviceIdType.MESH
F32 = jnp.float32
BF16 = jnp.bfloat16
NSEM = 192


def dot_t(a, b):
    return lax.dot_general(a, b, (((1,), (1,)), ((), ())), preferred_element_type=F32)


def t_dot(a, b):
    return lax.dot_general(a, b, (((0,), (0,)), ((), ())), preferred_element_type=F32)


def kernel(
    p_hbm, gain_hbm, w_hbm, qkg_hbm, cg_hbm,
    ctx_ref, ig_ref, wg_ref, small_ref,
    gain_ref, qkg_ref, cg_ref, xg, wv, nrm, nrm_t, proj, qkvg, mu, inv,
    cr, ci, ci1, t1, cxs_a, cxs_b, cxr_a, cxr_b, plane1_a, plane1_b, cys, cyr,
    ds, dr, dxr, dxl, dyx, dyy,
    sxs, sxr, trans, sms, smr,
    ss, rs, ls,
):
    d = lax.axis_index("dp")
    m = lax.axis_index("mp")
    xl, y, core = d // 8, (d // 2) % 4, d % 2
    xh, z = m // 8, m % 8
    count = [0]
    sends = []

    def at(xl_=None, y_=None, core_=None, xh_=None, z_=None):
        xl_ = xl if xl_ is None else xl_
        y_ = y if y_ is None else y_
        core_ = core if core_ is None else core_
        xh_ = xh if xh_ is None else xh_
        z_ = z if z_ is None else z_
        return {"dp": xl_ * 8 + y_ * 2 + core_, "mp": xh_ * 8 + z_}

    z_dev = {1: at(z_=(z + 1) % 8), -1: at(z_=(z + 7) % 8)}
    y_dev = {1: at(y_=(y + 1) % 4), -1: at(y_=(y + 3) % 4)}
    xh_dev = at(xh_=1 - xh)
    xl_dev = at(xl_=1 - xl)
    core_dev = at(core_=1 - core)

    def send(src, dst, dev):
        i = count[0]
        count[0] += 1
        copy = pltpu.make_async_remote_copy(
            src_ref=src, dst_ref=dst, send_sem=ss.at[i], recv_sem=rs.at[i],
            device_id=dev, device_id_type=MESH,
        )
        copy.start()
        sends.append(copy)
        return copy

    barrier = pltpu.get_barrier_semaphore()
    near = (z_dev[1], z_dev[-1], xh_dev, y_dev[1], y_dev[-1], xl_dev, core_dev)
    for other in near:
        pl.semaphore_signal(barrier, inc=1, device_id=other, device_id_type=MESH)
    own = [
        pltpu.make_async_copy(
            p_hbm.at[pl.ds(i * IMG, IMG)], xg.at[m, pl.ds(BASE[i], IMG)], ls.at[i])
        for i in range(NIMG)
    ]
    for c in own:
        c.start()
    weights = pltpu.make_async_copy(w_hbm, wv, ls.at[2])
    small_in = [
        pltpu.make_async_copy(a, b, ls.at[3 + i])
        for i, (a, b) in enumerate(((gain_hbm, gain_ref), (qkg_hbm, qkg_ref), (cg_hbm, cg_ref)))
    ]
    for c in small_in:
        c.start()
    weights.start()
    small_in[0].wait()
    gain = gain_ref[...].reshape(1, FB)
    xg[m, pl.ds(IMG, GR), :] = jnp.broadcast_to(gain, (GR, FB))
    pl.semaphore_wait(barrier, len(near))
    for c in own + small_in[1:]:
        c.wait()

    def blk(plane, zz):
        return (xh if plane == 0 else 1 - xh) * 8 + (zz + 16) % 8

    def span(img, part):
        lo0 = BASE[img]
        mid = lo0 + HALF
        end = lo0 + IMG + (GR if img == 0 else 0)
        return {
            "full": (lo0, end - lo0),
            "lo": (lo0, mid - lo0),
            "hi": (mid, end - mid),
            "hi0": (mid, HALF // 2),
            "hi1": (mid + HALF // 2, end - mid - HALF // 2),
        }[part]

    ring = {}
    xrecv = {0: [], 1: []}

    def send_block(img, plane, origin_z, part, dev):
        r, n = span(img, part)
        ref = xg.at[blk(plane, origin_z), pl.ds(r, n)]
        return send(ref, ref, dev)

    def hop_parts(plane):
        if plane == 0:
            return {1: "full", -1: "full"}, {1: "lo", -1: "hi"}
        return {1: "hi", -1: "hi"}, {1: "hi0", -1: "hi1"}

    def forward(img, plane, s):
        parts = hop_parts(plane)[0 if s < 4 else 1]
        for dr_ in (1, -1):
            ring[(img, plane, s, dr_)] = send_block(img, plane, z - (s - 1) * dr_, parts[dr_], z_dev[dr_])

    def arrive(img, plane, s):
        for dr_ in (1, -1):
            ring[(img, plane, s, dr_)].wait_recv()

    def ag0(img):
        ring[(img, "x")] = send_block(img, 0, z, "hi", xh_dev)
        forward(img, 0, 1)
        xrecv[img].append(send_block(img, 0, z, "lo", xh_dev))

    def ag1(img):
        ring[(img, "x")].wait_recv()
        forward(img, 1, 1)

    def ag_hop(img, plane, s):
        arrive(img, plane, s)
        if s < 4:
            forward(img, plane, s + 1)
        if plane == 0:
            for dr_ in (1, -1) if s < 4 else (1,):
                xrecv[img].append(send_block(img, 0, z - s * dr_, "lo", xh_dev))

    def ag_end(img):
        for c in xrecv[img]:
            c.wait_recv()

    def norm(img, half):
        @pl.loop(0, HALF // 64)
        def _(c):
            r = pl.ds(pl.multiple_of(BASE[img] + half * HALF + c * 64, 16), 64)
            shift = jnp.mean(xg[0, r, :].astype(F32), axis=1, keepdims=True)

            def stat(k, carry):
                v = xg[k, r, :].astype(F32) - shift
                w = v * v
                fold = lambda t: t[:, :128] + t[:, 128:256] + t[:, 256:]
                return carry[0] + fold(v), carry[1] + fold(w)

            zero = jnp.zeros((64, 128), F32)
            s1, s2 = lax.fori_loop(0, NB, stat, (zero, zero))
            off = jnp.sum(s1, axis=1, keepdims=True) / D
            var = jnp.sum(s2, axis=1, keepdims=True) / D - off * off
            mean = shift + off
            rstd = lax.rsqrt(jnp.maximum(var, 0.0) + EPS)
            mu[r, :] = mean
            inv[r, :] = rstd

            def put(k, _):
                g = xg[k, pl.ds(IMG, 1), :].astype(F32)
                unit = (xg[k, r, :].astype(F32) - mean) * rstd
                nrm[r, pl.ds(pl.multiple_of(k * FB, 128), FB)] = (unit * g).astype(BF16)
                return 0

            lax.fori_loop(0, NB, put, 0)

        if img == 0 and half == 1:
            @pl.loop(0, NB)
            def _(k):
                nrm[pl.ds(IMG, GR), pl.ds(pl.multiple_of(k * FB, 128), FB)] = xg[k, pl.ds(IMG, GR), :]

    def project(img):
        r = slice(0, BASE[1]) if img == 0 else slice(BASE[1], ROWS)

        @pl.loop(0, HC // 256)
        def _(c):
            cols = pl.ds(pl.multiple_of(c * 256, 256), 256)
            proj[r, cols] = jnp.dot(nrm[r, :], wv[:, cols], preferred_element_type=F32)

    def transpose(img):
        @pl.loop(0, NB)
        def _(k):
            cols = pl.ds(pl.multiple_of(k * FB, 128), FB)
            rows = slice(BASE[img], BASE[img] + IMG)
            nrm_t[cols, img * IMG:(img + 1) * IMG] = nrm[rows, cols].T

    def head_norm(v):
        cen = v - jnp.mean(v, axis=1, keepdims=True)
        rstd = lax.rsqrt(jnp.mean(cen * cen, axis=1, keepdims=True) + EPS)
        return cen * rstd, rstd

    def norm_back(g, unit, rstd):
        return rstd * (
            g - jnp.mean(g, axis=1, keepdims=True) - unit * jnp.mean(g * unit, axis=1, keepdims=True)
        )

    def attend(img, h):
        r = slice(BASE[img], BASE[img] + IMG)
        rows = slice(img * IMG, (img + 1) * IMG)
        c0 = h * 3 * HEAD_DIM
        cols = [slice(c0 + i * HEAD_DIM, c0 + (i + 1) * HEAD_DIM) for i in range(3)]
        q_gain, k_gain = qkg_ref[0, h:h + 1, :], qkg_ref[1, h:h + 1, :]
        q_unit, q_inv = head_norm(proj[r, cols[0]])
        k_unit, k_inv = head_norm(proj[r, cols[1]])
        qn = (q_unit * q_gain).astype(BF16)
        kn = (k_unit * k_gain).astype(BF16)
        v = proj[r, cols[2]].astype(BF16)
        hcols = slice(h * HEAD_DIM, (h + 1) * HEAD_DIM)
        cg = cg_ref[rows, hcols]
        sc = dot_t(qn, kn) * SCALE
        e = jnp.exp(sc - jnp.max(sc, axis=1, keepdims=True))
        probs = e * (1.0 / jnp.sum(e, axis=1, keepdims=True))
        low = probs.astype(BF16)
        ctx_ref[rows, hcols] = jnp.dot(low, v, preferred_element_type=F32).astype(BF16)
        dp = dot_t(cg, v)
        qkvg[rows, cols[2]] = t_dot(low, cg).astype(BF16)
        delta = jnp.sum(probs * dp, axis=1, keepdims=True)
        dsc = (probs * (dp - delta)).astype(BF16)
        dq = jnp.dot(dsc, kn, preferred_element_type=F32) * SCALE
        dk = t_dot(dsc, qn) * SCALE
        for i, (g, unit, rstd, gain) in enumerate(((dq, q_unit, q_inv, q_gain), (dk, k_unit, k_inv, k_gain))):
            part = jnp.sum(g * unit, axis=0, keepdims=True)
            row = slice(3 + 2 * i + h, 4 + 2 * i + h)
            if img > 0:
                part = part + sms[row, :]
            sms[row, :] = part
            qkvg[rows, cols[i]] = norm_back(g * gain, unit, rstd).astype(BF16)

    def sums(img):
        r = slice(BASE[img], BASE[img] + IMG)
        rows = slice(img * IMG, (img + 1) * IMG)
        g = qkvg[rows, :].astype(F32)
        one = jnp.sum(g * proj[IMG:IMG + 1, :], axis=1, keepdims=True)
        two = jnp.sum(g * proj[r, :], axis=1, keepdims=True)
        lane = lax.broadcasted_iota(jnp.int32, (IMG, 128), 1)
        both = jnp.where(lane == 0, one, jnp.where(lane == 1, two, 0.0))
        turned = both.T
        for i in range(2):
            for j in range(2):
                row = img * 4 + i * 2 + j
                sxs[row:row + 1, :] = turned[i:i + 1, j * 128:(j + 1) * 128]

    sx_copies = []

    def sums_send():
        for o in range(1, NB):
            sx_copies.append(send(sxs, sxr.at[m], {"dp": d, "mp": (m + o) % NB}))

    def sums_end():
        sxr[m] = sxs[...]
        for c in sx_copies:
            c.wait_recv()
        total = sxr[0]
        for k in range(1, NB):
            total = total + sxr[k]
        trans[...] = jnp.zeros_like(trans)
        for row in range(8):
            i, c = (row // 2) % 2, (row // 4) * IMG + (row % 2) * 128
            trans[i:i + 1, c:c + 128] = total[row:row + 1, :]

    cring = {}
    cx = {}

    def term(img, plane, zz):
        b = blk(plane, zz)
        w = wv[pl.ds(pl.multiple_of(b * FB, 16), FB), :]
        return dot_t(qkvg[img * IMG:(img + 1) * IMG, :], w)

    cxs, cxr, plane1 = (cxs_a, cxs_b), (cxr_a, cxr_b), (plane1_a, plane1_b)
    ORDER = (4, 3, 5, 2, 6, 1, 7, 0)

    def c_plane1(img, o):
        n = LOW[img]
        t = term(img, 1, z + o)
        cxs[img][o] = t[:n].astype(BF16)
        cx[(img, o)] = send(cxs[img].at[o], cxr[img].at[o], xh_dev)
        plane1[img][o] = t[n:].astype(BF16)

    def high(img, o):
        return plane1[img][o].astype(F32) if LOW[img] else term(img, 1, z + o)

    def c_start1(img):
        n = IMG - LOW[img]
        ci1[img, :n] = high(img, 4).astype(BF16)
        for i, dr_ in enumerate((1, -1)):
            part = pl.ds(i * n // 2, n // 2)
            cring[(img, 1, 1, dr_)] = send(ci1.at[img, part], t1.at[img, i, 0, part], z_dev[dr_])

    def c_add1(img, s):
        n = IMG - LOW[img]
        rows = pl.ds(0, n)
        for i, dr_ in enumerate((1, -1)):
            mine = high(img, (dr_ * (4 - s)) % 8)
            cring[(img, 1, s, dr_)].wait_recv()
            if s == 1:
                a = slice(i * n // 2, (i + 1) * n // 2)
                b = slice((1 - i) * n // 2, (2 - i) * n // 2)
                t1[img, i, 0, b] = mine[b].astype(BF16)
                t1[img, i, 0, a] = (mine[a] + t1[img, i, 0, a].astype(F32)).astype(BF16)
            else:
                t1[img, i, s - 1, :n] = (mine + t1[img, i, s - 1, :n].astype(F32)).astype(BF16)
            cring[(img, 1, s + 1, dr_)] = send(
                t1.at[img, i, s - 1, rows], t1.at[img, i, s, rows], z_dev[dr_])

    def c_end1(img):
        n = IMG - LOW[img]
        mine = high(img, 0)
        for dr_ in (1, -1):
            cring[(img, 1, 4, dr_)].wait_recv()
        tot = mine + t1[img, 0, 3, :n].astype(F32) + t1[img, 1, 3, :n].astype(F32)
        cys[img, :n] = tot.astype(BF16)
        cx[(img, "y")] = send(cys.at[img, pl.ds(0, n)], cyr.at[img, pl.ds(0, n)], xh_dev)

    def from_x(img, o):
        t = term(img, 0, z + o)
        n = LOW[img]
        if not n:
            return t
        cx[(img, o)].wait_recv()
        return jnp.concatenate([t[:n] + cxr[img][o].astype(F32), t[n:]], axis=0)

    def c_start0(img):
        ci[img] = from_x(img, 4).astype(BF16)
        for i, dr_ in enumerate((1, -1)):
            part = pl.ds(i * HALF, HALF)
            cring[(img, 0, 1, dr_)] = send(ci.at[img, part], cr.at[img, i, 0, part], z_dev[dr_])

    def c_add0(img, s):
        for i, dr_ in enumerate((1, -1)):
            t = from_x(img, (dr_ * (4 - s)) % 8)
            cring[(img, 0, s, dr_)].wait_recv()
            if s == 1:
                a, b = slice(i * HALF, (i + 1) * HALF), slice((1 - i) * HALF, (2 - i) * HALF)
                cr[img, i, 0, b] = t[b].astype(BF16)
                cr[img, i, 0, a] = (t[a] + cr[img, i, 0, a].astype(F32)).astype(BF16)
            else:
                cr[img, i, s - 1] = (t + cr[img, i, s - 1].astype(F32)).astype(BF16)
            cring[(img, 0, s + 1, dr_)] = send(cr.at[img, i, s - 1], cr.at[img, i, s], z_dev[dr_])

    def c_final(img):
        n = LOW[img]
        t = from_x(img, 0)
        for dr_ in (1, -1):
            cring[(img, 0, 4, dr_)].wait_recv()
        t = t + cr[img, 0, 3].astype(F32) + cr[img, 1, 3].astype(F32)
        cx[(img, "y")].wait_recv()
        rest = t[n:] + cyr[img, :IMG - n].astype(F32)
        ng = jnp.concatenate([t[:n], rest], axis=0) if n else rest
        cols = trans[:, img * IMG:(img + 1) * IMG].T
        r = slice(BASE[img], BASE[img] + IMG)
        rstd = inv[r, :]
        unit = (xg[m, r, :].astype(F32) - mu[r, :]) * rstd
        part = jnp.sum(ng * unit, axis=0, keepdims=True)
        back = ng * gain.astype(F32)
        res = rstd * (back - cols[:, 0:1] / D - unit * (cols[:, 1:2] / D))
        ig_ref[img * IMG:(img + 1) * IMG, :] = res.astype(BF16)
        for i in range(3):
            sms[i:i + 1, :] = sms[i:i + 1, :] + part[:, i * 128:(i + 1) * 128]

    dcore, dx, dy = {}, {}, {}

    def dest(a, b, same_core):
        xl_ = xl if a == 0 else 1 - xl
        return xl_ * 8 + ((y + b) % 4) * 2 + (core if same_core else 1 - core)

    def wgrad(a, b, same_core):
        k = dest(a, b, same_core)
        return jnp.dot(nrm_t[pl.ds(pl.multiple_of(k * FB, 16), FB), :], qkvg[...], preferred_element_type=F32)

    def d_core(a, b):
        j = a * 4 + b
        ds[j] = wgrad(a, b, False).astype(BF16)
        dcore[j] = send(ds.at[j], dr.at[j], core_dev)

    XS, YS = pl.ds(0, XC), pl.ds(XC, HC - XC)

    def y_buf(key):
        return dyx if key == 0 else dyy.at[key - 1]

    def y_start(key, ref, cols):
        for i, dr_ in enumerate((1, -1)):
            part = pl.ds(i * FB // 2, FB // 2)
            dy[(key, 1, dr_)] = send(ref.at[part, cols], y_buf(key).at[i, 0, part], y_dev[dr_])

    def d_own1(b):
        g = wgrad(1, b, True)
        j = 4 + b
        dcore[j].wait_recv()
        dr[j] = (g + dr[j].astype(F32)).astype(BF16)
        dx[b] = send(dr.at[j, :, XS], dxr.at[b], xl_dev)
        if b == 2:
            y_start(1, dr.at[j], YS)

    def d_own0(b):
        g = wgrad(0, b, True)
        dcore[b].wait_recv()
        dr[b] = (g + dr[b].astype(F32)).astype(BF16)
        if b == 2:
            y_start(2, dr.at[b], YS)

    def d_x0(b):
        dx[b].wait_recv()
        dr[b, :, :XC] = (dr[b, :, :XC].astype(F32) + dxr[b].astype(F32)).astype(BF16)
        if b == 2:
            y_start(0, dr.at[b], XS)

    def d_mid(key):
        cols = slice(0, XC) if key == 0 else slice(XC, HC)
        cds = XS if key == 0 else YS
        buf = y_buf(key)
        for i, dr_ in enumerate((1, -1)):
            j = (4 if key == 1 else 0) + (1 if i == 0 else 3)
            dy[(key, 1, dr_)].wait_recv()
            part = slice(i * FB // 2, (i + 1) * FB // 2)
            dr[j, part, cols] = (dr[j, part, cols].astype(F32) + buf[i, 0, part].astype(F32)).astype(BF16)
            dy[(key, 2, dr_)] = send(dr.at[j, :, cds], buf.at[i, 1], y_dev[dr_])

    def d_last(key):
        cols = slice(0, XC) if key == 0 else slice(XC, HC)
        buf = y_buf(key)
        for dr_ in (1, -1):
            dy[(key, 2, dr_)].wait_recv()
        j = 4 if key == 1 else 0
        tot = dr[j, :, cols].astype(F32) + buf[0, 1].astype(F32) + buf[1, 1].astype(F32)
        if key == 1:
            dr[j, :, cols] = tot.astype(BF16)
            dx["l"] = send(dr.at[j, :, YS], dxl, xl_dev)
        elif key == 0:
            wg_ref[:, cols] = tot.astype(BF16)
        else:
            dx["l"].wait_recv()
            wg_ref[:, cols] = (tot + dxl[...].astype(F32)).astype(BF16)

    def sums_start():
        sms[...] = jnp.zeros_like(sms)

    def small_send():
        for o in range(1, NB):
            sm_copies.append(send(sms, smr.at[d], {"dp": (d + o) % NB, "mp": m}))
        smr[d] = sms[...]

    def small_end():
        for c in sm_copies:
            c.wait_recv()
        total = smr[0]
        for k in range(1, NB):
            total = total + smr[k]
        small_ref[...] = total

    sm_copies = []
    steps = []

    def do(f, *a):
        steps.append((f, a))

    do(ag0, 0)
    do(ag1, 0)
    do(ag_hop, 0, 0, 1)
    do(ag_hop, 0, 1, 1)
    do(ag_hop, 0, 0, 2)
    do(ag_hop, 0, 1, 2)
    do(ag0, 1)
    do(ag_hop, 0, 1, 3)
    do(ag_hop, 0, 0, 3)
    do(ag_hop, 1, 0, 1)
    do(ag1, 1)
    do(sums_start)
    do(ag_hop, 0, 1, 4)
    do(ag_hop, 0, 0, 4)
    do(norm, 0, 1)
    do(ag_hop, 1, 0, 2)
    do(ag_end, 0)
    do(norm, 0, 0)
    do(ag_hop, 1, 1, 1)
    do(weights.wait)
    do(project, 0)
    do(ag_hop, 1, 0, 3)
    do(attend, 0, 0)
    do(ag_hop, 1, 1, 2)
    do(attend, 0, 1)
    do(c_plane1, 0, 4)
    do(c_start1, 0)
    do(transpose, 0)
    do(ag_hop, 1, 0, 4)
    do(c_plane1, 0, 3)
    do(c_plane1, 0, 5)
    do(ag_hop, 1, 1, 3)
    do(c_plane1, 0, 6)
    do(c_plane1, 0, 2)
    do(c_add1, 0, 1)
    do(c_plane1, 0, 0)
    do(c_start0, 0)
    do(c_plane1, 0, 7)
    do(ag_hop, 1, 1, 4)
    do(norm, 1, 1)
    do(ag_end, 1)
    do(norm, 1, 0)
    do(c_add1, 0, 2)
    do(transpose, 1)
    do(c_add0, 0, 1)
    do(project, 1)
    do(attend, 1, 0)
    do(attend, 1, 1)
    do(c_plane1, 1, 4)
    do(c_start1, 1)
    do(d_core, 1, 2)
    do(c_plane1, 0, 1)
    do(c_add1, 0, 3)
    do(d_core, 1, 3)
    do(c_add0, 0, 2)
    do(c_plane1, 1, 7)
    do(d_own1, 2)
    do(d_core, 0, 2)
    do(c_plane1, 1, 3)
    do(c_plane1, 1, 5)
    do(c_add1, 1, 1)
    do(c_start0, 1)
    do(c_plane1, 1, 2)
    do(sums, 1)
    do(c_plane1, 1, 6)
    do(d_core, 1, 1)
    do(d_own0, 2)
    do(sums, 0)
    do(c_end1, 0)
    do(d_own1, 3)
    do(d_own1, 1)
    do(d_x0, 2)
    do(d_core, 0, 3)
    do(c_add1, 1, 2)
    do(c_plane1, 1, 1)
    do(d_mid, 1)
    do(d_core, 1, 0)
    do(c_add0, 1, 1)
    do(sums_send)
    do(d_own1, 0)
    do(d_own0, 3)
    do(d_core, 0, 1)
    do(c_add1, 1, 3)
    do(d_core, 0, 0)
    do(c_add0, 1, 2)
    do(c_add0, 0, 3)
    do(c_plane1, 1, 0)
    do(c_end1, 1)
    do(d_x0, 3)
    do(d_own0, 1)
    do(d_x0, 1)
    do(d_mid, 0)
    do(d_own0, 0)
    do(d_x0, 0)
    do(d_last, 1)
    do(d_mid, 2)
    do(d_last, 0)
    do(c_add0, 1, 3)
    do(sums_end)
    do(c_final, 0)
    do(c_final, 1)
    do(small_send)
    do(d_last, 2)
    do(small_end)
    for f, a in steps:
        f(*a)
    for c in sends:
        c.wait_send()


def place(ctx, ig, wg, small, ctx_out, ig_out, wg_out, ngg_out, qkg_out):
    ctx_out[...] = ctx[...]
    ig_out[...] = ig[...]
    wg_out[...] = wg[...]
    for i in range(3):
        ngg_out[pl.ds(i * 128, 128)] = small[i, :]
    for i in range(2):
        qkg_out[i] = small[3 + 2 * i:5 + 2 * i, :]


def per_device(patches, norm_gain, qkv_weight, qk_gain, context_grad):
    vmem = pl.BlockSpec(memory_space=pltpu.VMEM)
    hbm = pl.BlockSpec(memory_space=pl.ANY)
    flops = 2 * TOK * D * HC * 3
    ctx, ig, wg, small = pl.pallas_call(
        kernel,
        out_shape=(
            jax.ShapeDtypeStruct((TOK, 256), BF16),
            jax.ShapeDtypeStruct((TOK, FB), BF16),
            jax.ShapeDtypeStruct((FB, HC), BF16),
            jax.ShapeDtypeStruct((8, 128), F32),
        ),
        in_specs=[hbm] * 5,
        out_specs=(vmem, vmem, vmem, vmem),
        scratch_shapes=[
            pltpu.VMEM((FB,), BF16),
            pltpu.VMEM((2, 2, HEAD_DIM), F32),
            pltpu.VMEM((TOK, 256), BF16),
            pltpu.VMEM((NB, ROWS, FB), BF16),
            pltpu.VMEM((D, HC), BF16),
            pltpu.VMEM((ROWS, D), BF16),
            pltpu.VMEM((D, TOK), BF16),
            pltpu.VMEM((ROWS, HC), F32),
            pltpu.VMEM((TOK, HC), BF16),
            pltpu.VMEM((ROWS, 1), F32),
            pltpu.VMEM((ROWS, 1), F32),
            pltpu.VMEM((NIMG, 2, 4, IMG, FB), BF16),
            pltpu.VMEM((NIMG, IMG, FB), BF16),
            pltpu.VMEM((NIMG, IMG, FB), BF16),
            pltpu.VMEM((NIMG, 2, 4, IMG, FB), BF16),
            *[pltpu.VMEM((8, max(n, 16), FB), BF16) for n in LOW],
            *[pltpu.VMEM((8, max(n, 16), FB), BF16) for n in LOW],
            *[pltpu.VMEM((8, IMG - n if n else 16, FB), BF16) for n in LOW],
            pltpu.VMEM((NIMG, IMG, FB), BF16),
            pltpu.VMEM((NIMG, IMG, FB), BF16),
            pltpu.VMEM((8, FB, HC), BF16),
            pltpu.VMEM((8, FB, HC), BF16),
            pltpu.VMEM((4, FB, XC), BF16),
            pltpu.VMEM((FB, HC - XC), BF16),
            pltpu.VMEM((2, 2, FB, XC), BF16),
            pltpu.VMEM((2, 2, 2, FB, HC - XC), BF16),
            pltpu.VMEM((8, 128), F32),
            pltpu.VMEM((NB, 8, 128), F32),
            pltpu.VMEM((128, TOK), F32),
            pltpu.VMEM((8, 128), F32),
            pltpu.VMEM((NB, 8, 128), F32),
            pltpu.SemaphoreType.DMA((NSEM,)),
            pltpu.SemaphoreType.DMA((NSEM,)),
            pltpu.SemaphoreType.DMA((6,)),
        ],
        compiler_params=pltpu.CompilerParams(
            collective_id=0, has_side_effects=True, vmem_limit_bytes=62 * 2**20
        ),
        cost_estimate=pl.CostEstimate(flops=flops, bytes_accessed=2**25, transcendentals=2**18),
    )(patches, norm_gain, qkv_weight, qk_gain, context_grad)
    return pl.pallas_call(
        place,
        out_shape=(
            jax.ShapeDtypeStruct((TOK, 256), BF16),
            jax.ShapeDtypeStruct((TOK, FB), BF16),
            jax.ShapeDtypeStruct((FB, HC), BF16),
            jax.ShapeDtypeStruct((FB,), F32),
            jax.ShapeDtypeStruct((2, 2, HEAD_DIM), F32),
        ),
        in_specs=[vmem] * 4,
        out_specs=(vmem,) * 5,
    )(ctx, ig, wg, small)


def solution(mesh):
    in_specs = (P("dp", "mp"), P("mp"), P(None, "mp"), P(None, "mp", None), P("dp", "mp"))
    out_specs = (P("dp", "mp"), P("dp", "mp"), P("dp", "mp"), P("mp"), P(None, "mp", None))
    return jax.shard_map(
        per_device, mesh=mesh, in_specs=in_specs, out_specs=out_specs, check_vma=False
    )
```

```python
import functools
import math

import jax
import jax.numpy as jnp
from jax import lax
from jax.experimental import pallas as pl
from jax.experimental.pallas import tpu as pltpu
from jax.sharding import PartitionSpec as P

HEAD_DIM = 128
IMG = 256
NIMG = 2
TOK = IMG * NIMG
FB = 384
NB = 16
D = FB * NB
HC = 768
GR = 16
ROWS = GR + TOK
HALF = IMG // 2
BASE = (0, IMG + GR)
XC = 128
MID = 384
STREAMS = ((0, 0, XC), (1, XC, MID), (0, XC, MID), (1, MID, HC), (0, MID, HC))
LOW = (128, 96)
EPS = 1e-6
SCALE = 1.0 / math.sqrt(HEAD_DIM)
MESH = pl.DeviceIdType.MESH
F32 = jnp.float32
BF16 = jnp.bfloat16
NSEM = 192


def dot_t(a, b):
    return lax.dot_general(a, b, (((1,), (1,)), ((), ())), preferred_element_type=F32)


def t_dot(a, b):
    return lax.dot_general(a, b, (((0,), (0,)), ((), ())), preferred_element_type=F32)


def kernel(
    p_hbm, gain_hbm, w_hbm, qkg_hbm, cg_hbm,
    ctx_hbm, ig_hbm, wg_hbm, small_hbm,
    ctx_ref, ig_ref, wg_ref, small_ref,
    gain_ref, qkg_ref, cg_ref, xg, wv, nrm, nrm_t, proj, qkvg, mu, inv,
    cr, ci, ci1, t1, cxs_a, cxs_b, cxr_a, cxr_b, plane1_a, plane1_b, cys, cyr,
    dr, dxr, dxl_a, dxl_b, dy_a, dy_b, dy_c, dy_d, dy_e,
    sxs, sxr, trans, sms, smr,
    ss, rs, ls,
):
    d = lax.axis_index("dp")
    m = lax.axis_index("mp")
    xl, y, core = d // 8, (d // 2) % 4, d % 2
    xh, z = m // 8, m % 8
    count = [0]
    sends = []
    outs = []

    def put_out(src, dst):
        c = pltpu.make_async_copy(src, dst, ls.at[6 + len(outs)])
        c.start()
        outs.append(c)

    def at(xl_=None, y_=None, core_=None, xh_=None, z_=None):
        xl_ = xl if xl_ is None else xl_
        y_ = y if y_ is None else y_
        core_ = core if core_ is None else core_
        xh_ = xh if xh_ is None else xh_
        z_ = z if z_ is None else z_
        return {"dp": xl_ * 8 + y_ * 2 + core_, "mp": xh_ * 8 + z_}

    z_dev = {1: at(z_=(z + 1) % 8), -1: at(z_=(z + 7) % 8)}
    y_dev = {1: at(y_=(y + 1) % 4), -1: at(y_=(y + 3) % 4)}
    xh_dev = at(xh_=1 - xh)
    xl_dev = at(xl_=1 - xl)
    core_dev = at(core_=1 - core)

    def send(src, dst, dev):
        i = count[0]
        count[0] += 1
        copy = pltpu.make_async_remote_copy(
            src_ref=src, dst_ref=dst, send_sem=ss.at[i], recv_sem=rs.at[i],
            device_id=dev, device_id_type=MESH,
        )
        copy.start()
        sends.append(copy)
        return copy

    barrier = pltpu.get_barrier_semaphore()
    near = (z_dev[1], z_dev[-1], xh_dev, y_dev[1], y_dev[-1], xl_dev, core_dev)
    for other in near:
        pl.semaphore_signal(barrier, inc=1, device_id=other, device_id_type=MESH)
    own = [
        pltpu.make_async_copy(
            p_hbm.at[pl.ds(i * IMG, IMG)], xg.at[m, pl.ds(BASE[i], IMG)], ls.at[i])
        for i in range(NIMG)
    ]
    for c in own:
        c.start()
    weights = pltpu.make_async_copy(w_hbm, wv, ls.at[2])
    small_in = [
        pltpu.make_async_copy(a, b, ls.at[3 + i])
        for i, (a, b) in enumerate(((gain_hbm, gain_ref), (qkg_hbm, qkg_ref), (cg_hbm, cg_ref)))
    ]
    for c in small_in:
        c.start()
    weights.start()
    small_in[0].wait()
    gain = gain_ref[...].reshape(1, FB)
    xg[m, pl.ds(IMG, GR), :] = jnp.broadcast_to(gain, (GR, FB))
    pl.semaphore_wait(barrier, len(near))
    for c in own + small_in[1:]:
        c.wait()

    def blk(plane, zz):
        return (xh if plane == 0 else 1 - xh) * 8 + (zz + 16) % 8

    def span(img, part):
        lo0 = BASE[img]
        mid = lo0 + HALF
        end = lo0 + IMG + (GR if img == 0 else 0)
        return {
            "full": (lo0, end - lo0),
            "lo": (lo0, mid - lo0),
            "hi": (mid, end - mid),
            "hi0": (mid, HALF // 2),
            "hi1": (mid + HALF // 2, end - mid - HALF // 2),
        }[part]

    ring = {}
    xrecv = {0: [], 1: []}

    def send_block(img, plane, origin_z, part, dev):
        r, n = span(img, part)
        ref = xg.at[blk(plane, origin_z), pl.ds(r, n)]
        return send(ref, ref, dev)

    def hop_parts(plane):
        if plane == 0:
            return {1: "full", -1: "full"}, {1: "lo", -1: "hi"}
        return {1: "hi", -1: "hi"}, {1: "hi0", -1: "hi1"}

    def forward(img, plane, s):
        parts = hop_parts(plane)[0 if s < 4 else 1]
        for dr_ in (1, -1):
            ring[(img, plane, s, dr_)] = send_block(img, plane, z - (s - 1) * dr_, parts[dr_], z_dev[dr_])

    def arrive(img, plane, s):
        for dr_ in (1, -1):
            ring[(img, plane, s, dr_)].wait_recv()

    def ag0(img):
        ring[(img, "x")] = send_block(img, 0, z, "hi", xh_dev)
        forward(img, 0, 1)
        xrecv[img].append(send_block(img, 0, z, "lo", xh_dev))

    def ag1(img):
        ring[(img, "x")].wait_recv()
        forward(img, 1, 1)

    def ag_hop(img, plane, s):
        arrive(img, plane, s)
        if s < 4:
            forward(img, plane, s + 1)
        if plane == 0:
            for dr_ in (1, -1) if s < 4 else (1,):
                xrecv[img].append(send_block(img, 0, z - s * dr_, "lo", xh_dev))

    def ag_end(img):
        for c in xrecv[img]:
            c.wait_recv()

    def norm(img, half):
        @pl.loop(0, HALF // 64)
        def _(c):
            r = pl.ds(pl.multiple_of(BASE[img] + half * HALF + c * 64, 16), 64)
            shift = jnp.mean(xg[0, r, :].astype(F32), axis=1, keepdims=True)

            def stat(k, carry):
                v = xg[k, r, :].astype(F32) - shift
                w = v * v
                fold = lambda t: t[:, :128] + t[:, 128:256] + t[:, 256:]
                return carry[0] + fold(v), carry[1] + fold(w)

            zero = jnp.zeros((64, 128), F32)
            s1, s2 = lax.fori_loop(0, NB, stat, (zero, zero))
            off = jnp.sum(s1, axis=1, keepdims=True) / D
            var = jnp.sum(s2, axis=1, keepdims=True) / D - off * off
            mean = shift + off
            rstd = lax.rsqrt(jnp.maximum(var, 0.0) + EPS)
            mu[r, :] = mean
            inv[r, :] = rstd

            def put(k, _):
                g = xg[k, pl.ds(IMG, 1), :].astype(F32)
                unit = (xg[k, r, :].astype(F32) - mean) * rstd
                nrm[r, pl.ds(pl.multiple_of(k * FB, 128), FB)] = (unit * g).astype(BF16)
                return 0

            lax.fori_loop(0, NB, put, 0)

        if img == 0 and half == 1:
            @pl.loop(0, NB)
            def _(k):
                nrm[pl.ds(IMG, GR), pl.ds(pl.multiple_of(k * FB, 128), FB)] = xg[k, pl.ds(IMG, GR), :]

    def project(img):
        r = slice(0, BASE[1]) if img == 0 else slice(BASE[1], ROWS)

        @pl.loop(0, HC // 256)
        def _(c):
            cols = pl.ds(pl.multiple_of(c * 256, 256), 256)
            proj[r, cols] = jnp.dot(nrm[r, :], wv[:, cols], preferred_element_type=F32)

    def transpose(img):
        @pl.loop(0, NB)
        def _(k):
            cols = pl.ds(pl.multiple_of(k * FB, 128), FB)
            rows = slice(BASE[img], BASE[img] + IMG)
            nrm_t[cols, img * IMG:(img + 1) * IMG] = nrm[rows, cols].T

    def head_norm(v):
        cen = v - jnp.mean(v, axis=1, keepdims=True)
        rstd = lax.rsqrt(jnp.mean(cen * cen, axis=1, keepdims=True) + EPS)
        return cen * rstd, rstd

    def norm_back(g, unit, rstd):
        return rstd * (
            g - jnp.mean(g, axis=1, keepdims=True) - unit * jnp.mean(g * unit, axis=1, keepdims=True)
        )

    def attend(img, h):
        r = slice(BASE[img], BASE[img] + IMG)
        rows = slice(img * IMG, (img + 1) * IMG)
        c0 = h * 3 * HEAD_DIM
        cols = [slice(c0 + i * HEAD_DIM, c0 + (i + 1) * HEAD_DIM) for i in range(3)]
        q_gain, k_gain = qkg_ref[0, h:h + 1, :], qkg_ref[1, h:h + 1, :]
        q_unit, q_inv = head_norm(proj[r, cols[0]])
        k_unit, k_inv = head_norm(proj[r, cols[1]])
        qn = (q_unit * q_gain).astype(BF16)
        kn = (k_unit * k_gain).astype(BF16)
        v = proj[r, cols[2]].astype(BF16)
        hcols = slice(h * HEAD_DIM, (h + 1) * HEAD_DIM)
        cg = cg_ref[rows, hcols]
        sc = dot_t(qn, kn) * SCALE
        e = jnp.exp(sc - jnp.max(sc, axis=1, keepdims=True))
        probs = e * (1.0 / jnp.sum(e, axis=1, keepdims=True))
        low = probs.astype(BF16)
        ctx_ref[rows, hcols] = jnp.dot(low, v, preferred_element_type=F32).astype(BF16)
        dp = dot_t(cg, v)
        qkvg[rows, cols[2]] = t_dot(low, cg).astype(BF16)
        delta = jnp.sum(probs * dp, axis=1, keepdims=True)
        dsc = (probs * (dp - delta)).astype(BF16)
        dq = jnp.dot(dsc, kn, preferred_element_type=F32) * SCALE
        dk = t_dot(dsc, qn) * SCALE
        for i, (g, unit, rstd, gain) in enumerate(((dq, q_unit, q_inv, q_gain), (dk, k_unit, k_inv, k_gain))):
            part = jnp.sum(g * unit, axis=0, keepdims=True)
            row = slice(3 + 2 * i + h, 4 + 2 * i + h)
            if img > 0:
                part = part + sms[row, :]
            sms[row, :] = part
            qkvg[rows, cols[i]] = norm_back(g * gain, unit, rstd).astype(BF16)

    def sums(img):
        r = slice(BASE[img], BASE[img] + IMG)
        rows = slice(img * IMG, (img + 1) * IMG)
        g = qkvg[rows, :].astype(F32)
        one = jnp.sum(g * proj[IMG:IMG + 1, :], axis=1, keepdims=True)
        two = jnp.sum(g * proj[r, :], axis=1, keepdims=True)
        lane = lax.broadcasted_iota(jnp.int32, (IMG, 128), 1)
        both = jnp.where(lane == 0, one, jnp.where(lane == 1, two, 0.0))
        turned = both.T
        for i in range(2):
            for j in range(2):
                row = img * 4 + i * 2 + j
                sxs[row:row + 1, :] = turned[i:i + 1, j * 128:(j + 1) * 128]

    sx_copies = []

    def sums_send():
        put_out(ctx_ref, ctx_hbm)
        for o in range(1, NB):
            sx_copies.append(send(sxs, sxr.at[m], {"dp": d, "mp": (m + o) % NB}))

    def sums_end():
        sxr[m] = sxs[...]
        for c in sx_copies:
            c.wait_recv()
        total = sxr[0]
        for k in range(1, NB):
            total = total + sxr[k]
        trans[...] = jnp.zeros_like(trans)
        for row in range(8):
            i, c = (row // 2) % 2, (row // 4) * IMG + (row % 2) * 128
            trans[i:i + 1, c:c + 128] = total[row:row + 1, :]

    cring = {}
    cx = {}

    def term(img, plane, zz):
        b = blk(plane, zz)
        w = wv[pl.ds(pl.multiple_of(b * FB, 16), FB), :]
        return dot_t(qkvg[img * IMG:(img + 1) * IMG, :], w)

    cxs, cxr, plane1 = (cxs_a, cxs_b), (cxr_a, cxr_b), (plane1_a, plane1_b)
    ORDER = (4, 3, 5, 2, 6, 1, 7, 0)

    def c_plane1(img, o):
        n = LOW[img]
        t = term(img, 1, z + o)
        cxs[img][o] = t[:n].astype(BF16)
        cx[(img, o)] = send(cxs[img].at[o], cxr[img].at[o], xh_dev)
        plane1[img][o] = t[n:].astype(BF16)

    def high(img, o):
        return plane1[img][o].astype(F32) if LOW[img] else term(img, 1, z + o)

    def c_start1(img):
        n = IMG - LOW[img]
        ci1[img, :n] = high(img, 4).astype(BF16)
        for i, dr_ in enumerate((1, -1)):
            part = pl.ds(i * n // 2, n // 2)
            cring[(img, 1, 1, dr_)] = send(ci1.at[img, part], t1.at[img, i, 0, part], z_dev[dr_])

    def c_add1(img, s):
        n = IMG - LOW[img]
        rows = pl.ds(0, n)
        for i, dr_ in enumerate((1, -1)):
            mine = high(img, (dr_ * (4 - s)) % 8)
            cring[(img, 1, s, dr_)].wait_recv()
            if s == 1:
                a = slice(i * n // 2, (i + 1) * n // 2)
                b = slice((1 - i) * n // 2, (2 - i) * n // 2)
                t1[img, i, 0, b] = mine[b].astype(BF16)
                t1[img, i, 0, a] = (mine[a] + t1[img, i, 0, a].astype(F32)).astype(BF16)
            else:
                t1[img, i, s - 1, :n] = (mine + t1[img, i, s - 1, :n].astype(F32)).astype(BF16)
            cring[(img, 1, s + 1, dr_)] = send(
                t1.at[img, i, s - 1, rows], t1.at[img, i, s, rows], z_dev[dr_])

    def c_end1(img):
        n = IMG - LOW[img]
        mine = high(img, 0)
        for dr_ in (1, -1):
            cring[(img, 1, 4, dr_)].wait_recv()
        tot = mine + t1[img, 0, 3, :n].astype(F32) + t1[img, 1, 3, :n].astype(F32)
        cys[img, :n] = tot.astype(BF16)
        cx[(img, "y")] = send(cys.at[img, pl.ds(0, n)], cyr.at[img, pl.ds(0, n)], xh_dev)

    def from_x(img, o):
        t = term(img, 0, z + o)
        n = LOW[img]
        if not n:
            return t
        cx[(img, o)].wait_recv()
        return jnp.concatenate([t[:n] + cxr[img][o].astype(F32), t[n:]], axis=0)

    def c_start0(img):
        ci[img] = from_x(img, 4).astype(BF16)
        for i, dr_ in enumerate((1, -1)):
            part = pl.ds(i * HALF, HALF)
            cring[(img, 0, 1, dr_)] = send(ci.at[img, part], cr.at[img, i, 0, part], z_dev[dr_])

    def c_add0(img, s):
        for i, dr_ in enumerate((1, -1)):
            t = from_x(img, (dr_ * (4 - s)) % 8)
            cring[(img, 0, s, dr_)].wait_recv()
            if s == 1:
                a, b = slice(i * HALF, (i + 1) * HALF), slice((1 - i) * HALF, (2 - i) * HALF)
                cr[img, i, 0, b] = t[b].astype(BF16)
                cr[img, i, 0, a] = (t[a] + cr[img, i, 0, a].astype(F32)).astype(BF16)
            else:
                cr[img, i, s - 1] = (t + cr[img, i, s - 1].astype(F32)).astype(BF16)
            cring[(img, 0, s + 1, dr_)] = send(cr.at[img, i, s - 1], cr.at[img, i, s], z_dev[dr_])

    def c_final(img):
        n = LOW[img]
        t = from_x(img, 0)
        for dr_ in (1, -1):
            cring[(img, 0, 4, dr_)].wait_recv()
        t = t + cr[img, 0, 3].astype(F32) + cr[img, 1, 3].astype(F32)
        cx[(img, "y")].wait_recv()
        rest = t[n:] + cyr[img, :IMG - n].astype(F32)
        ng = jnp.concatenate([t[:n], rest], axis=0) if n else rest
        cols = trans[:, img * IMG:(img + 1) * IMG].T
        r = slice(BASE[img], BASE[img] + IMG)
        rstd = inv[r, :]
        unit = (xg[m, r, :].astype(F32) - mu[r, :]) * rstd
        part = jnp.sum(ng * unit, axis=0, keepdims=True)
        back = ng * gain.astype(F32)
        res = rstd * (back - cols[:, 0:1] / D - unit * (cols[:, 1:2] / D))
        ig_ref[img * IMG:(img + 1) * IMG, :] = res.astype(BF16)
        part_rows = pl.ds(img * IMG, IMG)
        put_out(ig_ref.at[part_rows], ig_hbm.at[part_rows])
        for i in range(3):
            sms[i:i + 1, :] = sms[i:i + 1, :] + part[:, i * 128:(i + 1) * 128]

    dcore, dx, dy = {}, {}, {}

    def dest(a, b, same_core):
        xl_ = xl if a == 0 else 1 - xl
        return xl_ * 8 + ((y + b) % 4) * 2 + (core if same_core else 1 - core)

    def wgrad(a, b, same_core):
        k = dest(a, b, same_core)
        return jnp.dot(nrm_t[pl.ds(pl.multiple_of(k * FB, 16), FB), :], qkvg[...], preferred_element_type=F32)

    def d_core(a, b):
        j = a * 4 + b
        nrm[:FB, j * HC:(j + 1) * HC] = wgrad(a, b, False).astype(BF16)
        dcore[j] = send(nrm.at[pl.ds(0, FB), pl.ds(j * HC, HC)], dr.at[j], core_dev)

    XS = pl.ds(0, XC)
    ybuf = (dy_a, dy_b, dy_c, dy_d, dy_e)
    dxl = {1: dxl_a, 3: dxl_b}

    def y_start(key, j):
        _, c0, c1 = STREAMS[key]
        for i, dr_ in enumerate((1, -1)):
            part = pl.ds(i * FB // 2, FB // 2)
            dy[(key, 1, dr_)] = send(
                dr.at[j, part, pl.ds(c0, c1 - c0)], ybuf[key].at[i, 0, part], y_dev[dr_])

    def d_own1(b):
        g = wgrad(1, b, True)
        j = 4 + b
        dcore[j].wait_recv()
        dr[j] = (g + dr[j].astype(F32)).astype(BF16)
        dx[b] = send(dr.at[j, :, XS], dxr.at[b], xl_dev)
        if b == 2:
            y_start(1, j)
            y_start(3, j)

    def d_own0(b):
        g = wgrad(0, b, True)
        dcore[b].wait_recv()
        dr[b] = (g + dr[b].astype(F32)).astype(BF16)
        if b == 2:
            y_start(2, b)
            y_start(4, b)

    def d_x0(b):
        dx[b].wait_recv()
        dr[b, :, :XC] = (dr[b, :, :XC].astype(F32) + dxr[b].astype(F32)).astype(BF16)
        if b == 2:
            y_start(0, b)

    def d_mid(key):
        half, c0, c1 = STREAMS[key]
        buf = ybuf[key]
        for i, dr_ in enumerate((1, -1)):
            j = half * 4 + (1 if i == 0 else 3)
            dy[(key, 1, dr_)].wait_recv()
            part = slice(i * FB // 2, (i + 1) * FB // 2)
            dr[j, part, c0:c1] = (dr[j, part, c0:c1].astype(F32) + buf[i, 0, part].astype(F32)).astype(BF16)
            dy[(key, 2, dr_)] = send(dr.at[j, :, pl.ds(c0, c1 - c0)], buf.at[i, 1], y_dev[dr_])

    def d_last(key):
        half, c0, c1 = STREAMS[key]
        buf = ybuf[key]
        for dr_ in (1, -1):
            dy[(key, 2, dr_)].wait_recv()
        j = half * 4
        tot = dr[j, :, c0:c1].astype(F32) + buf[0, 1].astype(F32) + buf[1, 1].astype(F32)
        if half == 1:
            dr[j, :, c0:c1] = tot.astype(BF16)
            dx[("l", key)] = send(dr.at[j, :, pl.ds(c0, c1 - c0)], dxl[key], xl_dev)
            return
        if key > 0:
            dx[("l", key - 1)].wait_recv()
            tot = tot + dxl[key - 1][...].astype(F32)
        wg_ref[:, c0:c1] = tot.astype(BF16)
        put_out(wg_ref.at[:, pl.ds(c0, c1 - c0)], wg_hbm.at[:, pl.ds(c0, c1 - c0)])

    def sums_start():
        sms[...] = jnp.zeros_like(sms)

    def small_send():
        for o in range(1, NB):
            sm_copies.append(send(sms, smr.at[d], {"dp": (d + o) % NB, "mp": m}))
        smr[d] = sms[...]

    def small_end():
        for c in sm_copies:
            c.wait_recv()
        total = smr[0]
        for k in range(1, NB):
            total = total + smr[k]
        small_ref[...] = total
        put_out(small_ref, small_hbm)

    sm_copies = []
    steps = []

    def do(f, *a):
        steps.append((f, a))

    do(ag0, 0)
    do(ag1, 0)
    do(ag_hop, 0, 0, 1)
    do(ag_hop, 0, 1, 1)
    do(ag_hop, 0, 0, 2)
    do(ag_hop, 0, 1, 2)
    do(ag0, 1)
    do(ag_hop, 0, 1, 3)
    do(ag_hop, 0, 0, 3)
    do(ag_hop, 1, 0, 1)
    do(ag1, 1)
    do(sums_start)
    do(ag_hop, 0, 1, 4)
    do(ag_hop, 0, 0, 4)
    do(norm, 0, 1)
    do(ag_hop, 1, 0, 2)
    do(ag_end, 0)
    do(norm, 0, 0)
    do(ag_hop, 1, 1, 1)
    do(weights.wait)
    do(project, 0)
    do(ag_hop, 1, 0, 3)
    do(attend, 0, 0)
    do(ag_hop, 1, 1, 2)
    do(attend, 0, 1)
    do(c_plane1, 0, 4)
    do(c_start1, 0)
    do(transpose, 0)
    do(ag_hop, 1, 0, 4)
    do(c_plane1, 0, 3)
    do(c_plane1, 0, 5)
    do(ag_hop, 1, 1, 3)
    do(c_plane1, 0, 6)
    do(c_plane1, 0, 2)
    do(c_add1, 0, 1)
    do(c_plane1, 0, 0)
    do(c_start0, 0)
    do(c_plane1, 0, 7)
    do(ag_hop, 1, 1, 4)
    do(norm, 1, 1)
    do(ag_end, 1)
    do(norm, 1, 0)
    do(c_add1, 0, 2)
    do(transpose, 1)
    do(c_add0, 0, 1)
    do(project, 1)
    do(attend, 1, 0)
    do(attend, 1, 1)
    do(c_plane1, 1, 4)
    do(c_start1, 1)
    do(d_core, 1, 2)
    do(c_plane1, 0, 1)
    do(c_add1, 0, 3)
    do(d_core, 1, 3)
    do(c_add0, 0, 2)
    do(c_plane1, 1, 7)
    do(d_own1, 2)
    do(d_core, 0, 2)
    do(c_plane1, 1, 5)
    do(c_plane1, 1, 3)
    do(c_add1, 1, 1)
    do(d_core, 1, 1)
    do(c_start0, 1)
    do(c_plane1, 1, 2)
    do(sums, 1)
    do(c_plane1, 1, 6)
    do(d_own0, 2)
    do(sums, 0)
    do(c_end1, 0)
    do(d_own1, 3)
    do(d_own1, 1)
    do(d_x0, 2)
    do(d_core, 0, 3)
    do(c_add1, 1, 2)
    do(c_plane1, 1, 1)
    do(d_mid, 3)
    do(d_core, 1, 0)
    do(c_add0, 1, 1)
    do(sums_send)
    do(d_mid, 1)
    do(d_own1, 0)
    do(d_own0, 3)
    do(d_core, 0, 1)
    do(c_add1, 1, 3)
    do(d_core, 0, 0)
    do(c_add0, 1, 2)
    do(c_add0, 0, 3)
    do(c_plane1, 1, 0)
    do(c_end1, 1)
    do(d_x0, 3)
    do(d_own0, 1)
    do(d_x0, 1)
    do(d_mid, 0)
    do(d_own0, 0)
    do(d_x0, 0)
    do(d_last, 1)
    do(d_last, 3)
    do(d_mid, 2)
    do(d_mid, 4)
    do(d_last, 0)
    do(c_add0, 1, 3)
    do(sums_end)
    do(c_final, 0)
    do(c_final, 1)
    do(small_send)
    do(d_last, 2)
    do(d_last, 4)
    do(small_end)
    for f, a in steps:
        f(*a)
    for c in sends:
        c.wait_send()
    for c in outs:
        c.wait()


def place(ctx, ig, wg, small, ctx_out, ig_out, wg_out, ngg_out, qkg_out, ctx_v, ig_v, wg_v, small_v, ngg_v, qkg_v, sem):
    ins = [
        pltpu.make_async_copy(a, b, sem.at[i])
        for i, (a, b) in enumerate(((small, small_v), (wg, wg_v), (ig, ig_v), (ctx, ctx_v)))
    ]
    outs = [
        pltpu.make_async_copy(a, b, sem.at[4 + i])
        for i, (a, b) in enumerate(((wg_v, wg_out), (ig_v, ig_out), (ctx_v, ctx_out), (ngg_v, ngg_out), (qkg_v, qkg_out)))
    ]
    for c in ins:
        c.start()
    ins[0].wait()
    for i in range(3):
        ngg_v[pl.ds(i * 128, 128)] = small_v[i, :]
    for i in range(2):
        qkg_v[i] = small_v[3 + 2 * i:5 + 2 * i, :]
    outs[3].start()
    outs[4].start()
    for i in range(3):
        ins[1 + i].wait()
        outs[i].start()
    for c in outs:
        c.wait()


def per_device(patches, norm_gain, qkv_weight, qk_gain, context_grad):
    hbm = pl.BlockSpec(memory_space=pl.ANY)
    flops = 2 * TOK * D * HC * 3
    ctx, ig, wg, small = pl.pallas_call(
        kernel,
        out_shape=(
            jax.ShapeDtypeStruct((TOK, 256), BF16),
            jax.ShapeDtypeStruct((TOK, FB), BF16),
            jax.ShapeDtypeStruct((FB, HC), BF16),
            jax.ShapeDtypeStruct((8, 128), F32),
        ),
        in_specs=[hbm] * 5,
        out_specs=(hbm,) * 4,
        scratch_shapes=[
            pltpu.VMEM((TOK, 256), BF16),
            pltpu.VMEM((TOK, FB), BF16),
            pltpu.VMEM((FB, HC), BF16),
            pltpu.VMEM((8, 128), F32),
            pltpu.VMEM((FB,), BF16),
            pltpu.VMEM((2, 2, HEAD_DIM), F32),
            pltpu.VMEM((TOK, 256), BF16),
            pltpu.VMEM((NB, ROWS, FB), BF16),
            pltpu.VMEM((D, HC), BF16),
            pltpu.VMEM((ROWS, D), BF16),
            pltpu.VMEM((D, TOK), BF16),
            pltpu.VMEM((ROWS, HC), F32),
            pltpu.VMEM((TOK, HC), BF16),
            pltpu.VMEM((ROWS, 1), F32),
            pltpu.VMEM((ROWS, 1), F32),
            pltpu.VMEM((NIMG, 2, 4, IMG, FB), BF16),
            pltpu.VMEM((NIMG, IMG, FB), BF16),
            pltpu.VMEM((NIMG, IMG, FB), BF16),
            pltpu.VMEM((NIMG, 2, 4, IMG, FB), BF16),
            *[pltpu.VMEM((8, max(n, 16), FB), BF16) for n in LOW],
            *[pltpu.VMEM((8, max(n, 16), FB), BF16) for n in LOW],
            *[pltpu.VMEM((8, IMG - n if n else 16, FB), BF16) for n in LOW],
            pltpu.VMEM((NIMG, IMG, FB), BF16),
            pltpu.VMEM((NIMG, IMG, FB), BF16),
            pltpu.VMEM((8, FB, HC), BF16),
            pltpu.VMEM((4, FB, XC), BF16),
            pltpu.VMEM((FB, MID - XC), BF16),
            pltpu.VMEM((FB, HC - MID), BF16),
            *[pltpu.VMEM((2, 2, FB, c1 - c0), BF16) for _, c0, c1 in STREAMS],
            pltpu.VMEM((8, 128), F32),
            pltpu.VMEM((NB, 8, 128), F32),
            pltpu.VMEM((128, TOK), F32),
            pltpu.VMEM((8, 128), F32),
            pltpu.VMEM((NB, 8, 128), F32),
            pltpu.SemaphoreType.DMA((NSEM,)),
            pltpu.SemaphoreType.DMA((NSEM,)),
            pltpu.SemaphoreType.DMA((16,)),
        ],
        compiler_params=pltpu.CompilerParams(
            collective_id=0, has_side_effects=True, vmem_limit_bytes=58 * 2**20
        ),
        cost_estimate=pl.CostEstimate(flops=flops, bytes_accessed=2**25, transcendentals=2**18),
    )(patches, norm_gain, qkv_weight, qk_gain, context_grad)
    return pl.pallas_call(
        place,
        out_shape=(
            jax.ShapeDtypeStruct((TOK, 256), BF16),
            jax.ShapeDtypeStruct((TOK, FB), BF16),
            jax.ShapeDtypeStruct((FB, HC), BF16),
            jax.ShapeDtypeStruct((FB,), F32),
            jax.ShapeDtypeStruct((2, 2, HEAD_DIM), F32),
        ),
        in_specs=[hbm] * 4,
        out_specs=(hbm,) * 5,
        scratch_shapes=[
            pltpu.VMEM((TOK, 256), BF16),
            pltpu.VMEM((TOK, FB), BF16),
            pltpu.VMEM((FB, HC), BF16),
            pltpu.VMEM((8, 128), F32),
            pltpu.VMEM((FB,), F32),
            pltpu.VMEM((2, 2, HEAD_DIM), F32),
            pltpu.SemaphoreType.DMA((9,)),
        ],
    )(ctx, ig, wg, small)


def solution(mesh):
    in_specs = (P("dp", "mp"), P("mp"), P(None, "mp"), P(None, "mp", None), P("dp", "mp"))
    out_specs = (P("dp", "mp"), P("dp", "mp"), P("dp", "mp"), P("mp"), P(None, "mp", None))
    return jax.shard_map(
        per_device, mesh=mesh, in_specs=in_specs, out_specs=out_specs, check_vma=False
    )
```
